1024 devices in a mesh: fsdp: 128 (over x, y, z_lo), tp: 8 (over z_hi, core).
Axes of the slice: x: 8, y: 8, z: 8 (z_hi: 4, z_lo: 2; z = z_hi * 2 + z_lo), core: 2. Of those that a mesh axis runs over, the one named last changes fastest.
Arguments:
- acts: bfloat16 [32768, 128], P('fsdp'), may hold values from -24 to 24
- out_grad: bfloat16 [32768, 28672], P('fsdp', 'tp'), may hold values from -0.03125 to 0.03125
- moment: float32 [128, 28672], P('fsdp', 'tp'), may hold values from -4 to 4
- second: float32 [128, 28672], P('fsdp', 'tp'), may hold values from 0.01 to 1
- master: float32 [128, 28672], P('fsdp', 'tp'), may hold values from -0.5 to 0.5
- queries: bfloat16 [128, 64, 64, 128], P('fsdp', None, 'tp'), may hold values from -20 to 20
- cache_keys: bfloat16 [128, 1024, 8, 128], P('fsdp', None, 'tp'), may hold values from -6 to 6, as said below
- cache_values: bfloat16 [128, 1024, 8, 128], P('fsdp', None, 'tp'), may hold values from -6 to 6
- tree_keys: bfloat16 [128, 64, 8, 128], P('fsdp', None, 'tp'), may hold values from -6 to 6
- tree_values: bfloat16 [128, 64, 8, 128], P('fsdp', None, 'tp'), may hold values from -6 to 6
- parents: int32 [128, 64], P('fsdp'), may hold values from 0 to 62, as said below
- lengths: int32 [128], P('fsdp'), may hold values from 256 to 1024, as said below
- residual: bfloat16 [128, 64, 128], P('fsdp'), may hold values from -6 to 6
- out_proj: bfloat16 [8192, 128], P('tp'), may hold values from -0.75 to 0.75
Outputs:
- moment_new: float32 [128, 28672], P('fsdp', 'tp')
- second_new: float32 [128, 28672], P('fsdp', 'tp')
- master_new: float32 [128, 28672], P('fsdp', 'tp')
- proposal: bfloat16 [128, 64, 28672], P('fsdp', None, 'tp')
The draws below stay inside these ranges and needn't reach their ends.
Inputs may be any that keep to these rules, and one draw needn't show every extreme that they name: `cache_keys`: custom bfloat16 keys. parents[r, 0] = 0 (the root); for i >= 1, parents[r, i] < i. `lengths`: request 0 holds exactly 1024 cached tokens.
All inputs are finite; a program needn't handle non-finite values.
Results may differ from the reference program's by a relative error of at most 0.008.
Values may be sent and summed in bfloat16 or wider, within the bound.
A program may use at most 32 MiB of HBM per device.

```python
import math
import jax
import jax.numpy as jnp
from jax import lax

FF = 28672
HEADS = 64
KV_HEADS = 8
HEAD_DIM = 128
ROWS = 128
CACHE = 1024
NODES = 64
TOKENS = 32768
REQUESTS = 128


def draw_queries(key, part):
    key = jax.random.fold_in(key, 11)
    shape = (REQUESTS, NODES, HEADS, HEAD_DIM)
    values = jnp.clip(jax.random.normal(key, shape, jnp.float32), -6.0, 6.0)
    return values.astype(jnp.bfloat16)


def draw_cache_keys(key, part):
    key = jax.random.fold_in(key, 12)
    shape = (REQUESTS, CACHE, KV_HEADS, HEAD_DIM)
    values = jnp.clip(jax.random.normal(key, shape, jnp.float32), -6.0, 6.0)
    return values.astype(jnp.bfloat16)


def draw_parents(key, part):
    key = jax.random.fold_in(key, 17)
    upper = jnp.maximum(jnp.arange(NODES, dtype=jnp.int32), 1)
    return jax.random.randint(key, (REQUESTS, NODES), 0, upper[None, :]).astype(jnp.int32)


def draw_lengths(key, part):
    key = jax.random.fold_in(key, 13)
    drawn = jax.random.randint(key, (REQUESTS,), CACHE // 4, CACHE + 1)
    return drawn.at[0].set(CACHE).astype(jnp.int32)


def spiked(values, own_key, source, target, shards_of, factor):
    def block_of(dim):
        return (jnp.arange(values.shape[dim]) // (values.shape[dim] // shards_of)).reshape((-1,) + (1,) * (values.ndim - 1 - dim))

    near = jax.random.permutation(own_key, shards_of)[block_of(target)]
    second = (block_of(target) + shards_of // 2) % shards_of
    return jnp.where((block_of(source) == near) | (block_of(source) == second), factor * values, values)


def shard_levels(key, dims, shards, smallest, high):
    def one(axis_at, blocks):
        steps = jax.random.uniform(jax.random.fold_in(jax.random.fold_in(key, 6), axis_at), (blocks,), jnp.float32, smallest / len(shards), high / len(shards))
        return jnp.repeat(jnp.exp(steps), dims[axis_at] // blocks).reshape((-1,) + (1,) * (len(dims) - axis_at - 1))

    loudness = one(*shards[0])
    for cut in shards[1:]:
        loudness = loudness * one(*cut)
    return loudness


def bell_draw(own_key, dims, width, bound, shards=(), kind=jnp.bfloat16):
    result = jax.random.normal(own_key, dims, jnp.float32) * width
    if len(shards) > 0:
        result = shard_levels(own_key, dims, shards, -0.22, 0.18) * result
    return jnp.clip(result, min=-bound, max=bound).astype(kind)


def gaussian_with(own_key, dims, spread, bound, pieces, heavy, kind=jnp.bfloat16):
    array = spread * jax.random.normal(own_key, dims, jnp.float32)
    if pieces:
        array = array * shard_levels(own_key, dims, pieces, -0.22, 0.18)
    return jnp.clip(spiked(array, jax.random.fold_in(own_key, 3), *heavy), -bound, bound).astype(kind)


def setup_inputs(seed: int = 0) -> dict:
    streams_of = jax.random.split(jax.random.key(seed), 15)
    return {
        "acts": gaussian_with(streams_of[0], (TOKENS, ROWS), 1.0, 24.0, ((0, 128),), (0, 1, 128, 5.5)),
        "out_grad": bell_draw(streams_of[1], (TOKENS, FF), TOKENS ** -0.5, 0.03125, ((0, 128), (1, 8))),
        "moment": bell_draw(streams_of[2], (ROWS, FF), 0.3, 4.0, ((0, 128), (1, 8)), jnp.float32),
        "second": jnp.clip(jnp.exp(math.log(1.0) - 4.6051702 * jax.random.uniform(streams_of[3], (ROWS, FF), jnp.float32) ** shard_levels(streams_of[3], (ROWS, FF), ((0, 128), (1, 8)), -0.2, 0.2)), 0.01, 1.0),
        "master": bell_draw(streams_of[4], (ROWS, FF), ROWS ** -0.5, 0.5, ((0, 128), (1, 8)), jnp.float32),
        "queries": draw_queries(jax.random.fold_in(streams_of[14], 71), 0),
        "cache_keys": draw_cache_keys(jax.random.fold_in(streams_of[14], 71), 0),
        "cache_values": bell_draw(streams_of[7], (REQUESTS, CACHE, KV_HEADS, HEAD_DIM), 1.0, 6.0, ((0, 128), (2, 8))),
        "tree_keys": bell_draw(streams_of[8], (REQUESTS, NODES, KV_HEADS, HEAD_DIM), 1.0, 6.0, ((0, 128), (2, 8))),
        "tree_values": bell_draw(streams_of[9], (REQUESTS, NODES, KV_HEADS, HEAD_DIM), 1.0, 6.0, ((0, 128), (2, 8))),
        "parents": draw_parents(jax.random.fold_in(streams_of[14], 71), 0),
        "lengths": draw_lengths(jax.random.fold_in(streams_of[14], 71), 0),
        "residual": bell_draw(streams_of[12], (REQUESTS, NODES, ROWS), 0.5, 6.0, ((0, 128),)),
        "out_proj": bell_draw(streams_of[13], (HEADS * HEAD_DIM, ROWS), (HEAD_DIM // 2) ** -0.5, 0.75, ((0, 8),)),
    }


beta_one = 0.9
beta_two = 0.95
adam_eps = 1e-08
learn_rate = 0.001
weight_decay = 0.1
adam_count = 10
masked_score = -1e+30

def ancestry(parent_row):
    nodes = parent_row.shape[0]
    positions = jnp.arange(nodes, dtype=jnp.int32)
    links = ((positions[None, :] == parent_row[:, None]) & (positions[:, None] > 0)).astype(jnp.float32)
    reach = jnp.eye(nodes, dtype=jnp.float32) + links
    for sweep in range(max(1, (nodes - 1).bit_length())):
        reach = jnp.minimum(jnp.dot(reach, reach, preferred_element_type=jnp.float32), 1.0)
    return reach

def tree_attend(query, cache_k, cache_v, tree_k, tree_v, length, parent_row):
    nodes, heads, depth = query.shape
    kv_heads = cache_k.shape[1]
    group = heads // kv_heads
    score_scale = depth ** (-0.5)
    grouped = query.astype(jnp.float32).reshape(nodes, kv_heads, group, depth)
    cache_scores = jnp.einsum('nkgd,ckd->kgnc', grouped, cache_k.astype(jnp.float32)) * score_scale
    tree_scores = jnp.einsum('nkgd,mkd->kgnm', grouped, tree_k.astype(jnp.float32)) * score_scale
    live = jnp.arange(cache_k.shape[0], dtype=jnp.int32) < length
    cache_scores = jnp.where(live, cache_scores, masked_score)
    tree_scores = jnp.where(ancestry(parent_row) > 0.5, tree_scores, masked_score)
    row_top = jnp.maximum(lax.optimization_barrier(jnp.max(cache_scores, -1, keepdims=True)), lax.optimization_barrier(jnp.max(tree_scores, -1, keepdims=True)))
    cache_exp = jnp.exp(cache_scores - row_top)
    tree_exp = jnp.exp(tree_scores - row_top)
    total = lax.optimization_barrier(jnp.sum(cache_exp, -1, keepdims=True)) + lax.optimization_barrier(jnp.sum(tree_exp, -1, keepdims=True))
    cache_weights = (cache_exp / total).astype(jnp.bfloat16)
    tree_weights = (tree_exp / total).astype(jnp.bfloat16)
    mixed = jnp.einsum('kgnc,ckd->nkgd', cache_weights.astype(jnp.float32), cache_v.astype(jnp.float32))
    mixed = mixed + jnp.einsum('kgnm,mkd->nkgd', tree_weights.astype(jnp.float32), tree_v.astype(jnp.float32))
    return mixed.reshape(nodes, heads * depth).astype(jnp.bfloat16)

def reference(acts, out_grad, moment, second, master, queries, cache_keys, cache_values, tree_keys, tree_values, parents, lengths, residual, out_proj):
    gradient = jnp.dot(acts.T, out_grad, preferred_element_type=jnp.float32)
    moment_new = beta_one * moment + (1.0 - beta_one) * gradient
    second_new = beta_two * second + (1.0 - beta_two) * gradient * gradient
    corr_one = 1.0 - beta_one ** adam_count
    corr_two = 1.0 - beta_two ** adam_count
    direction = moment_new / corr_one / (jnp.sqrt(second_new / corr_two) + adam_eps)
    master_new = master - learn_rate * (direction + weight_decay * master)
    rollout = master_new.astype(jnp.bfloat16)

    def attend_one(items):
        return tree_attend(*items)
    attended = lax.map(attend_one, (queries, cache_keys, cache_values, tree_keys, tree_values, lengths, parents))
    requests, nodes = (queries.shape[0], queries.shape[1])
    head_out = jnp.dot(attended.reshape(requests * nodes, -1), out_proj, preferred_element_type=jnp.float32)
    hidden = (residual.reshape(requests * nodes, -1).astype(jnp.float32) + head_out).astype(jnp.bfloat16)
    proposal = jnp.dot(hidden, rollout, preferred_element_type=jnp.float32).astype(jnp.bfloat16)
    return (moment_new, second_new, master_new, proposal.reshape(requests, nodes, -1))
```

```python
import functools

import jax
import jax.numpy as jnp
from jax import lax
from jax.experimental import pallas as pl
from jax.experimental.pallas import tpu as pltpu
from jax.sharding import PartitionSpec as P

beta_one = 0.9
beta_two = 0.95
adam_eps = 1e-08
learn_rate = 0.001
weight_decay = 0.1
adam_count = 10
masked_score = -1e30

MESH = pl.DeviceIdType.MESH
LANES = 128
GRIDS = {128: (8, 8, 2), 32: (4, 4, 2), 16: (4, 4, 1), 8: (2, 2, 2)}


def nt_dot(a, b):
    return lax.dot_general(a, b, (((1,), (1,)), ((), ())), preferred_element_type=jnp.float32)


def dot(a, b):
    return jnp.dot(a, b, preferred_element_type=jnp.float32)


def kernel(
    cfg,
    acts_h,
    og_h,
    mom_h,
    sec_h,
    mas_h,
    q_h,
    k_h,
    v_h,
    tk_h,
    tv_h,
    par_h,
    len_s,
    res_h,
    op_h,
    mom_o,
    sec_o,
    mas_o,
    prop_o,
    acts,
    og,
    opt,
    q,
    k,
    v,
    tk,
    tv,
    par,
    res,
    op,
    grad,
    rs_out,
    rs_in,
    tile_f,
    tile_out,
    tile_in,
    row_all,
    roll,
    qf,
    ht,
    pair_in,
    quad,
    hid,
    opt_new,
    own,
    stage,
    load_sem,
    store_sem,
    rs_send,
    rs_recv,
    ex_send,
    ex_recv,
    row_send,
    row_recv,
    ag_send,
    ag_recv,
    tp_send,
    tp_recv,
):
    nx, ny, nz, nq, chunks = cfg
    rows = acts.shape[1]
    width = grad.shape[-1]
    tiles = width // LANES * chunks
    pad = tile_f.shape[0] // (rows // nx)
    nodes = res.shape[0]
    heads = q.shape[0] // nodes
    half_nodes = nodes // 2

    f = lax.axis_index("fsdp")
    t = lax.axis_index("tp")
    x, y, z = f // (ny * nz), lax.rem(f // nz, ny), lax.rem(f, nz)
    core, zh = lax.rem(t, 2), t // 2
    sides = (nx, ny)
    pos = (x, y)
    group = (ny * nz, nx * nz)
    mine = (y * nz + z, x * nz + z)

    def ring_peer(a, step):
        if a == 0:
            return (lax.rem(x + step + nx, nx) * ny + y) * nz + z
        return (x * ny + lax.rem(y + step + ny, ny)) * nz + z

    def group_peer(a, j):
        if a == 0:
            return x * (ny * nz) + j
        return ((j // nz) * ny + y) * nz + lax.rem(j, nz)

    loads = {}

    def load(name, src, dst):
        copy = pltpu.make_async_copy(src, dst, load_sem.at[len(loads)])
        copy.start()
        loads[name] = copy

    load("acts", acts_h, acts)
    for c in range(chunks):
        for a in range(2):
            base = (a * chunks + c) * width
            load(("og", a, c), og_h.at[:, pl.ds(base, width)], og.at[a, c])
    load("par", par_h, par)
    load("q", q_h, q)
    load("tk", tk_h, tk)
    load("k", k_h, k)
    load("v", v_h, v)
    load("tv", tv_h, tv)
    load("op", op_h, op)
    load("res", res_h, res)
    load("mom", mom_h, opt.at[0])
    load("sec", sec_h, opt.at[1])
    load("mas", mas_h, opt.at[2])

    barrier = pltpu.get_barrier_semaphore()
    count = 0
    for kk in range(1, group[0]):
        j = lax.rem(mine[0] + kk, group[0])
        pl.semaphore_signal(barrier, inc=1, device_id=(group_peer(0, j), t), device_id_type=MESH)
        count += 1
    for xx in range(1, nx):
        for zz in range(nz):
            j = lax.rem(x + xx, nx) * nz + zz
            pl.semaphore_signal(barrier, inc=1, device_id=(group_peer(1, j), t), device_id_type=MESH)
            count += 1
    sibling = zh * 2 + 1 - core
    pl.semaphore_signal(barrier, inc=1, device_id=(f, sibling), device_id_type=MESH)
    count += 1
    for kk in range(1, nq):
        peer = lax.rem(zh + kk, nq) * 2 + core
        pl.semaphore_signal(barrier, inc=1, device_id=(f, peer), device_id_type=MESH)
        count += 1

    tile_f[...] = jnp.zeros_like(tile_f)

    row_at = lax.broadcasted_iota(jnp.int32, (rows, rows), 0)
    col_at = lax.broadcasted_iota(jnp.int32, (rows, rows), 1)
    py, px, pz = row_at // (nx * nz), lax.rem(row_at // nz, nx), lax.rem(row_at, nz)
    swap = (col_at == (px * ny + py) * nz + pz).astype(jnp.bfloat16)
    same = (col_at == row_at).astype(jnp.bfloat16)
    loads["acts"].wait()
    acts_t = [nt_dot(same, acts[...]).astype(jnp.bfloat16), nt_dot(swap, acts[...]).astype(jnp.bfloat16)]

    started = []

    def block(a, target):
        return pl.ds(pl.multiple_of(target * (rows // sides[a]), rows // sides[a]), rows // sides[a])

    def rs_copy(a, d, s, c):
        sign = 1 - 2 * d
        return pltpu.make_async_remote_copy(
            src_ref=rs_out.at[a, d, s, c],
            dst_ref=rs_in.at[a, d, s, c],
            send_sem=rs_send.at[a, d, s, c],
            recv_sem=rs_recv.at[a, d, s, c],
            device_id=(ring_peer(a, sign), t),
            device_id_type=MESH,
        )

    def rs_step(a, d, s, c):
        n = sides[a]
        sign = 1 - 2 * d
        target = lax.rem(pos[a] + sign * (n // 2 - s) + n, n)
        value = grad[a, c, block(a, target), :]
        if s > 1 or (s == 1 and c % 2 == d):
            rs_copy(a, d, s - 1, c).wait_recv()
            value = value + rs_in[a, d, s - 1, c].astype(jnp.float32)
        rs_out[a, d, s, c] = value.astype(jnp.bfloat16)
        copy = rs_copy(a, d, s, c)
        copy.start()
        started.append(copy)

    first = True
    for c in range(chunks):
        for a in range(2):
            loads[("og", a, c)].wait()
            grad[a, c] = dot(acts_t[a], og[a, c])
            if first:
                pl.semaphore_wait(barrier, count)
                first = False
            rs_step(a, c % 2, 0, c)

    loads["par"].wait()
    j_at = lax.broadcasted_iota(jnp.int32, (nodes, nodes), 0)
    i_at = lax.broadcasted_iota(jnp.int32, (nodes, nodes), 1)
    links = ((par[...] == j_at) & (i_at > 0)) | (i_at == j_at)
    reach = links.astype(jnp.bfloat16)
    for _ in range(max(1, (nodes - 1).bit_length())):
        reach = jnp.minimum(dot(reach, reach), 1.0).astype(jnp.bfloat16)
    pick_row = lax.broadcasted_iota(jnp.int32, (2 * nodes, nodes), 0)
    pick_col = lax.broadcasted_iota(jnp.int32, (2 * nodes, nodes), 1)
    pick = (lax.rem(pick_row, nodes) == pick_col).astype(jnp.bfloat16)
    admitted = nt_dot(pick, reach) > 0.5
    loads["q"].wait()
    qf[...] = q[...].astype(jnp.float32)

    depth = q.shape[1]
    scale = depth ** (-0.5)

    def attend(u):
        if u == 0:
            loads["tk"].wait()
            loads["k"].wait()
        pair = jnp.concatenate(
            [qf[pl.ds(2 * u + e, nodes, stride=heads), :] for e in range(2)], axis=0
        ).astype(jnp.bfloat16)
        s_cache = nt_dot(pair, k[...])
        s_tree = nt_dot(pair, tk[...])
        live = lax.broadcasted_iota(jnp.int32, s_cache.shape, 1) < len_s[0]
        s_cache = jnp.where(live, s_cache, masked_score)
        s_tree = jnp.where(admitted, s_tree, masked_score)
        top = jnp.maximum(
            jnp.max(s_cache, axis=1, keepdims=True), jnp.max(s_tree, axis=1, keepdims=True)
        )
        e_cache = jnp.exp((s_cache - top) * scale)
        e_tree = jnp.exp((s_tree - top) * scale)
        total = jnp.sum(e_cache, axis=1, keepdims=True) + jnp.sum(e_tree, axis=1, keepdims=True)
        if u == 0:
            loads["v"].wait()
            loads["tv"].wait()
            loads["op"].wait()
        mixed = dot(e_cache.astype(jnp.bfloat16), v[...]) + dot(e_tree.astype(jnp.bfloat16), tv[...])
        mixed = (mixed / total).astype(jnp.bfloat16)
        add = dot(mixed[:nodes], op[pl.ds(2 * u * depth, depth), :]) + dot(
            mixed[nodes:], op[pl.ds((2 * u + 1) * depth, depth), :]
        )
        if u == 0:
            ht[...] = add
        else:
            ht[...] += add

    unit = 0
    units = heads // 2
    steps = max(nx, ny) // 2
    for s in range(1, steps):
        for c in range(chunks):
            for a in range(2):
                for d in range(2):
                    if s < sides[a] // 2:
                        rs_step(a, d, s, c)
        if unit < units:
            attend(unit)
            unit += 1
    while unit < units:
        attend(unit)
        unit += 1

    own_nodes = pl.ds(pl.multiple_of(core * half_nodes, half_nodes), half_nodes)
    other_nodes = pl.ds(pl.multiple_of((1 - core) * half_nodes, half_nodes), half_nodes)
    pair_copy = pltpu.make_async_remote_copy(
        src_ref=ht.at[other_nodes],
        dst_ref=pair_in,
        send_sem=tp_send.at[0],
        recv_sem=tp_recv.at[0],
        device_id=(f, sibling),
        device_id_type=MESH,
    )
    pair_copy.start()

    ex_copies = []
    for a in range(2):
        n = sides[a]
        last = n // 2 - 1
        for c in range(chunks):
            value = grad[a, c, block(a, pos[a]), :]
            for d in range(2):
                if last > 0 or c % 2 == d:
                    rs_copy(a, d, last, c).wait_recv()
                    value = value + rs_in[a, d, last, c].astype(jnp.float32)
            for e in range(width // LANES):
                at = c * (width // LANES) + e
                tile_f[pl.ds(at, group[a], stride=pad), :] = value[:, e * LANES : (e + 1) * LANES]
        tile_out[a] = tile_f[...].astype(jnp.bfloat16).reshape(group[a], pad, LANES)
        own[a] = tile_f[pl.ds(pl.multiple_of(mine[a] * pad, pad), pad), :]
        for kk in range(1, group[a]):
            j = lax.rem(mine[a] + kk, group[a])
            copy = pltpu.make_async_remote_copy(
                src_ref=tile_out.at[a, j],
                dst_ref=tile_in.at[a, kk - 1],
                send_sem=ex_send.at[a],
                recv_sem=ex_recv.at[a],
                device_id=(group_peer(a, j), t),
                device_id_type=MESH,
            )
            copy.start()
            ex_copies.append(copy)

    pair_copy.wait_recv()
    quad[zh] = ht[own_nodes, :] + pair_in[...]
    quad_copies = []
    for kk in range(1, nq):
        copy = pltpu.make_async_remote_copy(
            src_ref=quad.at[zh],
            dst_ref=quad.at[zh],
            send_sem=tp_send.at[kk],
            recv_sem=tp_recv.at[kk],
            device_id=(f, lax.rem(zh + kk, nq) * 2 + core),
            device_id_type=MESH,
        )
        copy.start()
        quad_copies.append(copy)

    for name in ("mom", "sec", "mas"):
        loads[name].wait()
    corr_one = 1.0 - beta_one**adam_count
    corr_two = 1.0 - beta_two**adam_count
    for a in range(2):
        pltpu.make_async_copy(
            tile_in.at[a, pl.ds(0, group[a] - 1)], tile_in.at[a, pl.ds(0, group[a] - 1)], ex_recv.at[a]
        ).wait()
        g = own[a]
        for kk in range(group[a] - 1):
            g = g + tile_in[a, kk].astype(jnp.float32)
        g = g[:tiles]
        part = pl.ds(a * tiles, tiles)
        moment_new = beta_one * opt[0, part, :] + (1.0 - beta_one) * g
        second_new = beta_two * opt[1, part, :] + (1.0 - beta_two) * g * g
        direction = moment_new / corr_one / (jnp.sqrt(second_new / corr_two) + adam_eps)
        master = opt[2, part, :]
        master_new = master - learn_rate * (direction + weight_decay * master)
        fill = jnp.zeros((pad - tiles, LANES), jnp.float32)
        row_all[a, mine[a]] = jnp.concatenate([master_new, fill], axis=0).astype(jnp.bfloat16)
        for kk in range(1, group[a]):
            j = lax.rem(mine[a] + kk, group[a])
            copy = pltpu.make_async_remote_copy(
                src_ref=row_all.at[a, mine[a]],
                dst_ref=row_all.at[a, mine[a]],
                send_sem=row_send.at[a],
                recv_sem=row_recv.at[a],
                device_id=(group_peer(a, j), t),
                device_id_type=MESH,
            )
            copy.start()
        opt_new[0, part, :] = moment_new
        opt_new[1, part, :] = second_new
        opt_new[2, part, :] = master_new

    stores = []

    def store(src, dst):
        copy = pltpu.make_async_copy(src, dst, store_sem.at[len(stores)])
        copy.start()
        stores.append(copy)

    store(opt_new.at[0], mom_o)
    store(opt_new.at[1], sec_o)
    store(opt_new.at[2], mas_o)

    loads["res"].wait()
    for copy in quad_copies:
        copy.wait_recv()
    head_out = quad[0]
    for kk in range(1, nq):
        head_out = head_out + quad[kk]
    hid[own_nodes, :] = (res[own_nodes, :].astype(jnp.float32) + head_out).astype(jnp.bfloat16)
    hid_copy = pltpu.make_async_remote_copy(
        src_ref=hid.at[own_nodes],
        dst_ref=hid.at[own_nodes],
        send_sem=tp_send.at[nq],
        recv_sem=tp_recv.at[nq],
        device_id=(f, sibling),
        device_id_type=MESH,
    )
    hid_copy.start()

    def ag_copy(a, d, s, c):
        n = sides[a]
        sign = 1 - 2 * d
        owner = lax.rem(pos[a] - sign * s + n, n)
        ref = roll.at[a, c, block(a, owner)]
        return pltpu.make_async_remote_copy(
            src_ref=ref,
            dst_ref=ref,
            send_sem=ag_send.at[a, d, s, c],
            recv_sem=ag_recv.at[a, d, s, c],
            device_id=(ring_peer(a, sign), t),
            device_id_type=MESH,
        )

    def ag_used(a, d, s, c):
        return s < sides[a] // 2 - 1 or (s == sides[a] // 2 - 1 and c % 2 == d)

    def ag_wait(a, d, s, c):
        n = sides[a]
        sign = 1 - 2 * d
        owner = lax.rem(pos[a] - sign * (s + 1) + n, n)
        ref = roll.at[a, c, block(a, owner)]
        pltpu.make_async_remote_copy(
            src_ref=ref,
            dst_ref=ref,
            send_sem=ag_send.at[a, d, s, c],
            recv_sem=ag_recv.at[a, d, s, c],
            device_id=(ring_peer(a, sign), t),
            device_id_type=MESH,
        ).wait_recv()

    def ag_start(a, d, s, c):
        copy = ag_copy(a, d, s, c)
        copy.start()
        started.append(copy)

    for a in range(2):
        pltpu.make_async_copy(
            row_all.at[a, pl.ds(0, group[a] - 1)], row_all.at[a, pl.ds(0, group[a] - 1)], row_recv.at[a]
        ).wait()
        tile_f[...] = row_all[a].astype(jnp.float32).reshape(group[a] * pad, LANES)
        for c in range(chunks):
            for e in range(width // LANES):
                at = c * (width // LANES) + e
                roll[a, c, block(a, pos[a]), pl.ds(e * LANES, LANES)] = tile_f[
                    pl.ds(at, group[a], stride=pad), :
                ].astype(jnp.bfloat16)
            for d in range(2):
                if ag_used(a, d, 0, c):
                    ag_start(a, d, 0, c)
    for s in range(1, steps):
        for c in range(chunks):
            for a in range(2):
                for d in range(2):
                    if ag_used(a, d, s - 1, c):
                        ag_wait(a, d, s - 1, c)
                        if ag_used(a, d, s, c):
                            ag_start(a, d, s, c)

    hid_copy.wait_recv()
    hidden = hid[...]
    hiddens = (hidden, nt_dot(hidden, swap).astype(jnp.bfloat16))

    for c in range(chunks):
        for a in range(2):
            for d in range(2):
                last = sides[a] // 2 - 1
                if ag_used(a, d, last, c):
                    ag_wait(a, d, last, c)
            stage[a, c] = dot(hiddens[a], roll[a, c]).astype(jnp.bfloat16)
            store(stage.at[a, c], prop_o.at[:, pl.ds((a * chunks + c) * width, width)])

    for copy in started:
        copy.wait_send()
    for a in range(2):
        pltpu.make_async_copy(
            tile_out.at[a, pl.ds(0, group[a] - 1)], tile_out.at[a, pl.ds(0, group[a] - 1)], ex_send.at[a]
        ).wait()
        pltpu.make_async_copy(
            row_all.at[a, pl.ds(0, group[a] - 1)], row_all.at[a, pl.ds(0, group[a] - 1)], row_send.at[a]
        ).wait()
    pair_copy.wait_send()
    for copy in quad_copies:
        copy.wait_send()
    hid_copy.wait_send()
    for copy in stores:
        copy.wait()


def local(
    acts,
    out_grad,
    moment,
    second,
    master,
    queries,
    cache_keys,
    cache_values,
    tree_keys,
    tree_values,
    parents,
    lengths,
    residual,
    out_proj,
    *,
    grid,
    nq,
):
    nx, ny, nz = grid
    chunks = 2
    rows = acts.shape[1]
    columns = out_grad.shape[1]
    width = columns // (2 * chunks)
    tiles = width // LANES * chunks
    pad = -(-tiles // 16) * 16
    nodes, heads, depth = queries.shape[1:]
    cache = cache_keys.shape[1]
    side = ny * nz
    steps = nx // 2
    bf16, f32 = jnp.bfloat16, jnp.float32
    any_spec = pl.BlockSpec(memory_space=pl.ANY)
    dma = pltpu.SemaphoreType.DMA
    moment_new, second_new, master_new, proposal = pl.pallas_call(
        functools.partial(kernel, (nx, ny, nz, nq, chunks)),
        out_shape=[jax.ShapeDtypeStruct((2 * tiles, LANES), f32)] * 3
        + [jax.ShapeDtypeStruct((nodes, columns), bf16)],
        in_specs=[any_spec] * 11 + [pl.BlockSpec(memory_space=pltpu.SMEM)] + [any_spec] * 2,
        out_specs=[any_spec] * 4,
        scratch_shapes=[
            pltpu.VMEM(acts.shape, bf16),
            pltpu.VMEM((2, chunks, acts.shape[0], width), bf16),
            pltpu.VMEM((3, 2 * tiles, LANES), f32),
            pltpu.VMEM((nodes * heads, depth), bf16),
            pltpu.VMEM((cache, depth), bf16),
            pltpu.VMEM((cache, depth), bf16),
            pltpu.VMEM((nodes, depth), bf16),
            pltpu.VMEM((nodes, depth), bf16),
            pltpu.VMEM((1, nodes), jnp.int32),
            pltpu.VMEM((nodes, rows), bf16),
            pltpu.VMEM(out_proj.shape, bf16),
            pltpu.VMEM((2, chunks, rows, width), f32),
            pltpu.VMEM((2, 2, steps, chunks, side, width), bf16),
            pltpu.VMEM((2, 2, steps, chunks, side, width), bf16),
            pltpu.VMEM((side * pad, LANES), f32),
            pltpu.VMEM((2, side, pad, LANES), bf16),
            pltpu.VMEM((2, side - 1, pad, LANES), bf16),
            pltpu.VMEM((2, side, pad, LANES), bf16),
            pltpu.VMEM((2, chunks, rows, width), bf16),
            pltpu.VMEM((nodes * heads, depth), f32),
            pltpu.VMEM((nodes, rows), f32),
            pltpu.VMEM((nodes // 2, rows), f32),
            pltpu.VMEM((nq, nodes // 2, rows), f32),
            pltpu.VMEM((nodes, rows), bf16),
            pltpu.VMEM((3, 2 * tiles, LANES), f32),
            pltpu.VMEM((2, pad, LANES), f32),
            pltpu.VMEM((2, chunks, nodes, width), bf16),
            dma((12 + 2 * chunks,)),
            dma((3 + 2 * chunks,)),
            dma((2, 2, steps, chunks)),
            dma((2, 2, steps, chunks)),
            dma((2,)),
            dma((2,)),
            dma((2,)),
            dma((2,)),
            dma((2, 2, steps, chunks)),
            dma((2, 2, steps, chunks)),
            dma((nq + 1,)),
            dma((nq + 1,)),
        ],
        compiler_params=pltpu.CompilerParams(
            collective_id=0, has_side_effects=True, vmem_limit_bytes=44 * 1024 * 1024
        ),
    )(
        acts,
        out_grad,
        moment.reshape(2 * tiles, LANES),
        second.reshape(2 * tiles, LANES),
        master.reshape(2 * tiles, LANES),
        queries.reshape(nodes * heads, depth),
        cache_keys.reshape(cache, depth),
        cache_values.reshape(cache, depth),
        tree_keys.reshape(nodes, depth),
        tree_values.reshape(nodes, depth),
        parents,
        lengths,
        residual.reshape(nodes, rows),
        out_proj,
    )
    return (
        moment_new.reshape(moment.shape),
        second_new.reshape(second.shape),
        master_new.reshape(master.shape),
        proposal.reshape(1, nodes, columns),
    )


def solution(mesh):
    in_specs = (
        P("fsdp", None),
        P("fsdp", "tp"),
        P("fsdp", "tp"),
        P("fsdp", "tp"),
        P("fsdp", "tp"),
        P("fsdp", None, "tp", None),
        P("fsdp", None, "tp", None),
        P("fsdp", None, "tp", None),
        P("fsdp", None, "tp", None),
        P("fsdp", None, "tp", None),
        P("fsdp", None),
        P("fsdp"),
        P("fsdp", None, None),
        P("tp", None),
    )
    out_specs = (P("fsdp", "tp"), P("fsdp", "tp"), P("fsdp", "tp"), P("fsdp", None, "tp"))
    body = functools.partial(local, grid=GRIDS[mesh.shape["fsdp"]], nq=mesh.shape["tp"] // 2)
    return jax.shard_map(body, mesh=mesh, in_specs=in_specs, out_specs=out_specs, check_vma=False)
```

```python
import functools

import jax
import jax.numpy as jnp
from jax import lax
from jax.experimental import pallas as pl
from jax.experimental.pallas import tpu as pltpu
from jax.sharding import PartitionSpec as P

beta_one = 0.9
beta_two = 0.95
adam_eps = 1e-08
learn_rate = 0.001
weight_decay = 0.1
adam_count = 10
masked_score = -1e30

MESH = pl.DeviceIdType.MESH
LANES = 128
GRIDS = {128: (8, 8, 2), 32: (4, 4, 2), 16: (4, 4, 1), 8: (2, 2, 2)}


def nt_dot(a, b):
    return lax.dot_general(a, b, (((1,), (1,)), ((), ())), preferred_element_type=jnp.float32)


def dot(a, b):
    return jnp.dot(a, b, preferred_element_type=jnp.float32)


def adam(g, moment, second, master):
    moment_new = beta_one * moment + (1.0 - beta_one) * g
    second_new = beta_two * second + (1.0 - beta_two) * g * g
    corr_one = 1.0 - beta_one**adam_count
    corr_two = 1.0 - beta_two**adam_count
    direction = moment_new / corr_one / (jnp.sqrt(second_new / corr_two) + adam_eps)
    master_new = master - learn_rate * (direction + weight_decay * master)
    return moment_new, second_new, master_new


def step_kernel(
    cfg,
    acts_h,
    og_h,
    mom_h,
    sec_h,
    mas_h,
    q_h,
    k_h,
    v_h,
    tk_h,
    tv_h,
    par_h,
    len_h,
    res_h,
    op_h,
    g_o,
    hid_o,
    roll_o,
    acts,
    og,
    opt,
    opt_t,
    q,
    k,
    v,
    tk,
    tv,
    par,
    length,
    res,
    op,
    grad,
    rs_out,
    rs_in,
    tile_f,
    tile_out,
    tile_in,
    row_all,
    blk,
    qf,
    ht,
    ht_in,
    head_all,
    hid,
    g_row,
    own,
    load_sem,
    store_sem,
    rs_send,
    rs_recv,
    ex_send,
    ex_recv,
    row_send,
    row_recv,
    ag_send,
    ag_recv,
    tp_send,
    tp_recv,
):
    nx, ny, nz, nt, chunks = cfg
    rows = acts.shape[1]
    width = grad.shape[-1]
    per = width // LANES
    tiles = per * chunks
    pad = tile_out.shape[2]
    nodes = res.shape[0]
    heads = q.shape[0] // nodes
    share = nodes // nt

    f = lax.axis_index("fsdp")
    t = lax.axis_index("tp")
    x, y, z = f // (ny * nz), lax.rem(f // nz, ny), lax.rem(f, nz)
    sides = (nx, ny)
    pos = (x, y)
    group = (ny * nz, nx * nz)
    mine = (y * nz + z, x * nz + z)

    def line_peer(a, at):
        if a == 0:
            return (at * ny + y) * nz + z
        return (x * ny + at) * nz + z

    def group_peer(a, j):
        if a == 0:
            return x * (ny * nz) + j
        return ((j // nz) * ny + y) * nz + lax.rem(j, nz)

    def far_first(n):
        return sorted(range(1, n), key=lambda kk: -min(kk, n - kk))

    loads = {}

    def load(name, src, dst):
        copy = pltpu.make_async_copy(src, dst, load_sem.at[len(loads)])
        copy.start()
        loads[name] = copy

    load("acts", acts_h, acts)
    for c in range(chunks):
        for a in range(2):
            base = (a * chunks + c) * width
            load(("og", a, c), og_h.at[:, pl.ds(base, width)], og.at[a, c])

    barrier = pltpu.get_barrier_semaphore()
    count = 0
    for kk in range(1, group[0]):
        j = lax.rem(mine[0] + kk, group[0])
        pl.semaphore_signal(barrier, inc=1, device_id=(group_peer(0, j), t), device_id_type=MESH)
        count += 1
    for xx in range(1, nx):
        for zz in range(nz):
            j = lax.rem(x + xx, nx) * nz + zz
            pl.semaphore_signal(barrier, inc=1, device_id=(group_peer(1, j), t), device_id_type=MESH)
            count += 1
    for kk in range(1, nt):
        pl.semaphore_signal(barrier, inc=1, device_id=(f, lax.rem(t + kk, nt)), device_id_type=MESH)
        count += 1

    row_at = lax.broadcasted_iota(jnp.int32, (rows, rows), 0)
    col_at = lax.broadcasted_iota(jnp.int32, (rows, rows), 1)
    py, px, pz = row_at // (nx * nz), lax.rem(row_at // nz, nx), lax.rem(row_at, nz)
    swap = (col_at == (px * ny + py) * nz + pz).astype(jnp.bfloat16)
    same = (col_at == row_at).astype(jnp.bfloat16)
    loads["acts"].wait()
    acts_t = [nt_dot(m, acts[...]).astype(jnp.bfloat16) for m in (same, swap)]

    def block(a, at):
        depth = rows // sides[a]
        return pl.ds(pl.multiple_of(at * depth, depth), depth)

    def wait_for(ref, sem):
        pltpu.make_async_copy(ref, ref, sem).wait()

    for c in range(chunks):
        for a in range(2):
            n = sides[a]
            loads[("og", a, c)].wait()
            value = dot(acts_t[a], og[a, c])
            grad[a, c] = value
            rs_out[a, c] = value.astype(jnp.bfloat16)
            if c == 0 and a == 0:
                pl.semaphore_wait(barrier, count)
            for kk in far_first(n):
                at = lax.rem(pos[a] + kk, n)
                pltpu.make_async_remote_copy(
                    src_ref=rs_out.at[a, c, block(a, at)],
                    dst_ref=rs_in.at[a, c, kk - 1],
                    send_sem=rs_send.at[a, c],
                    recv_sem=rs_recv.at[a, c],
                    device_id=(line_peer(a, at), t),
                    device_id_type=MESH,
                ).start()

    load("par", par_h, par)
    load("q", q_h, q)
    load("tk", tk_h, tk)
    load("k", k_h, k)
    load("len", len_h, length)
    load("v", v_h, v)
    load("tv", tv_h, tv)
    load("op", op_h, op)
    load("mom", mom_h, opt.at[0])
    load("sec", sec_h, opt.at[1])
    load("mas", mas_h, opt.at[2])
    load("res", res_h, res)
    tile_f[...] = jnp.zeros_like(tile_f)

    loads["par"].wait()
    j_at = lax.broadcasted_iota(jnp.int32, (nodes, nodes), 0)
    i_at = lax.broadcasted_iota(jnp.int32, (nodes, nodes), 1)
    links = ((par[...] == j_at) & (i_at > 0)) | (i_at == j_at)
    reach = links.astype(jnp.bfloat16)
    for _ in range(max(1, (nodes - 1).bit_length())):
        reach = jnp.minimum(dot(reach, reach), 1.0).astype(jnp.bfloat16)
    pick_row = lax.broadcasted_iota(jnp.int32, (2 * nodes, nodes), 0)
    pick_col = lax.broadcasted_iota(jnp.int32, (2 * nodes, nodes), 1)
    pick = (lax.rem(pick_row, nodes) == pick_col).astype(jnp.bfloat16)
    admitted = nt_dot(pick, reach) > 0.5
    loads["q"].wait()
    qf[...] = q[...].astype(jnp.float32)

    depth = q.shape[1]
    scale = depth ** (-0.5)
    for name in ("tk", "k", "len", "v", "tv", "op"):
        loads[name].wait()

    def attend(u):
        pair = jnp.concatenate(
            [qf[pl.ds(2 * u + e, nodes, stride=heads), :] for e in range(2)], axis=0
        ).astype(jnp.bfloat16)
        s_cache = nt_dot(pair, k[...])
        s_tree = nt_dot(pair, tk[...])
        live = lax.broadcasted_iota(jnp.int32, s_cache.shape, 1) < length[...]
        s_cache = jnp.where(live, s_cache, masked_score)
        s_tree = jnp.where(admitted, s_tree, masked_score)
        top = jnp.maximum(
            jnp.max(s_cache, axis=1, keepdims=True), jnp.max(s_tree, axis=1, keepdims=True)
        )
        e_cache = jnp.exp((s_cache - top) * scale)
        e_tree = jnp.exp((s_tree - top) * scale)
        total = jnp.sum(e_cache, axis=1, keepdims=True) + jnp.sum(e_tree, axis=1, keepdims=True)
        mixed = dot(e_cache.astype(jnp.bfloat16), v[...]) + dot(e_tree.astype(jnp.bfloat16), tv[...])
        mixed = (mixed / total).astype(jnp.bfloat16)
        add = dot(mixed[:nodes], op[pl.ds(2 * u * depth, depth), :]) + dot(
            mixed[nodes:], op[pl.ds((2 * u + 1) * depth, depth), :]
        )
        if u == 0:
            ht[...] = add
        else:
            ht[...] += add

    units = heads // 2
    early = units - 1
    for u in range(early):
        attend(u)

    for i, name in enumerate(("mom", "sec", "mas")):
        loads[name].wait()
        for a in range(2):
            for e in range(tiles):
                opt_t[i, a, pl.ds(e, 1), :] = opt[i, :, pl.ds((a * tiles + e) * LANES, LANES)]
    loads["res"].wait()

    for a in range(2):
        n = sides[a]
        for c in range(chunks):
            wait_for(rs_in.at[a, c], rs_recv.at[a, c])
            value = grad[a, c, block(a, pos[a]), :]
            for kk in range(n - 1):
                value = value + rs_in[a, c, kk].astype(jnp.float32)
            for e in range(per):
                tile_f[a, pl.ds(c * per + e, group[a], stride=pad), :] = value[:, e * LANES : (e + 1) * LANES]
        tile_out[a] = tile_f[a].astype(jnp.bfloat16).reshape(group[a], pad, LANES)
        for kk in far_first(group[a]):
            j = lax.rem(mine[a] + kk, group[a])
            pltpu.make_async_remote_copy(
                src_ref=tile_out.at[a, j],
                dst_ref=tile_in.at[a, kk - 1],
                send_sem=ex_send.at[a],
                recv_sem=ex_recv.at[a],
                device_id=(group_peer(a, j), t),
                device_id_type=MESH,
            ).start()
        own[a] = tile_f[a, pl.ds(pl.multiple_of(mine[a] * pad, pad), pad), :]

    for u in range(early, units):
        attend(u)

    def share_of(at):
        return pl.ds(pl.multiple_of(at * share, share), share)

    for kk in range(1, nt):
        at = lax.rem(t + kk, nt)
        pltpu.make_async_remote_copy(
            src_ref=ht.at[share_of(at)],
            dst_ref=ht_in.at[kk - 1],
            send_sem=tp_send.at[0],
            recv_sem=tp_recv.at[0],
            device_id=(f, at),
            device_id_type=MESH,
        ).start()

    g_tiles = []
    for a in range(2):
        wait_for(tile_in.at[a], ex_recv.at[a])
        g = own[a]
        for kk in range(group[a] - 1):
            g = g + tile_in[a, kk].astype(jnp.float32)
        g = g[:tiles]
        g_tiles.append(g)
        master_new = adam(g, opt_t[0, a], opt_t[1, a], opt_t[2, a])[2]
        if pad > tiles:
            fill = jnp.zeros((pad - tiles, LANES), jnp.float32)
            master_new = jnp.concatenate([master_new, fill], axis=0)
        row_all[a, mine[a]] = master_new.astype(jnp.bfloat16)
        for kk in far_first(group[a]):
            j = lax.rem(mine[a] + kk, group[a])
            pltpu.make_async_remote_copy(
                src_ref=row_all.at[a, mine[a]],
                dst_ref=row_all.at[a, mine[a]],
                send_sem=row_send.at[a],
                recv_sem=row_recv.at[a],
                device_id=(group_peer(a, j), t),
                device_id_type=MESH,
            ).start()

    stores = []

    def store(src, dst):
        copy = pltpu.make_async_copy(src, dst, store_sem.at[len(stores)])
        copy.start()
        stores.append(copy)

    for a in range(2):
        for e in range(tiles):
            g_row[:, pl.ds((a * tiles + e) * LANES, LANES)] = g_tiles[a][e : e + 1]
    store(g_row, g_o)

    wait_for(ht_in, tp_recv.at[0])
    head = ht[share_of(t), :]
    for kk in range(nt - 1):
        head = head + ht_in[kk]
    head_all[share_of(t), :] = head
    for kk in range(1, nt):
        pltpu.make_async_remote_copy(
            src_ref=head_all.at[share_of(t)],
            dst_ref=head_all.at[share_of(t)],
            send_sem=tp_send.at[1],
            recv_sem=tp_recv.at[1],
            device_id=(f, lax.rem(t + kk, nt)),
            device_id_type=MESH,
        ).start()

    for a in range(2):
        n = sides[a]
        wait_for(row_all.at[a, pl.ds(0, group[a] - 1)], row_recv.at[a])
        tile_f[a] = row_all[a].astype(jnp.float32).reshape(group[a] * pad, LANES)
        for c in range(chunks):
            for e in range(per):
                blk[a, c, :, pl.ds(e * LANES, LANES)] = tile_f[
                    a, pl.ds(c * per + e, group[a], stride=pad), :
                ].astype(jnp.bfloat16)
            for kk in far_first(n):
                at = lax.rem(pos[a] + kk, n)
                pltpu.make_async_remote_copy(
                    src_ref=blk.at[a, c],
                    dst_ref=roll_o.at[a, c, block(a, pos[a])],
                    send_sem=ag_send.at[a, c],
                    recv_sem=ag_recv.at[a, c],
                    device_id=(line_peer(a, at), t),
                    device_id_type=MESH,
                ).start()
            store(blk.at[a, c], roll_o.at[a, c, block(a, pos[a])])

    wait_for(head_all.at[pl.ds(0, (nt - 1) * share)], tp_recv.at[1])
    hidden = (res[...].astype(jnp.float32) + head_all[...]).astype(jnp.bfloat16)
    hid[0] = hidden
    hid[1] = nt_dot(hidden, swap).astype(jnp.bfloat16)
    store(hid, hid_o)

    for a in range(2):
        for c in range(chunks):
            wait_for(rs_in.at[a, c], rs_send.at[a, c])
        wait_for(tile_in.at[a], ex_send.at[a])
        wait_for(row_all.at[a, pl.ds(0, group[a] - 1)], row_send.at[a])
    wait_for(ht_in, tp_send.at[0])
    wait_for(head_all.at[pl.ds(0, (nt - 1) * share)], tp_send.at[1])
    for a in range(2):
        n = sides[a]
        for c in range(chunks):
            others = pl.ds(0, rows - rows // n)
            wait_for(roll_o.at[a, c, others], ag_send.at[a, c])
            wait_for(roll_o.at[a, c, others], ag_recv.at[a, c])
    for copy in stores:
        copy.wait()


def result_kernel(
    roll_h, hid_h, g_h, mom_h, sec_h, mas_h, mom_o, sec_o, mas_o, prop_o, roll, hid, opt, opt_new, stage, load_sem, store_sem
):
    halves, chunks, _, width = roll.shape
    loads = [pltpu.make_async_copy(hid_h, hid, load_sem.at[0])]
    for i in range(halves * chunks):
        at = (i // chunks, i % chunks)
        loads.append(pltpu.make_async_copy(roll_h.at[at], roll.at[at], load_sem.at[1 + i]))
    for i, ref in enumerate((g_h, mom_h, sec_h, mas_h)):
        loads.append(pltpu.make_async_copy(ref, opt.at[i], load_sem.at[1 + halves * chunks + i]))
    for copy in loads:
        copy.start()
    stores = []
    loads[0].wait()
    for i in range(halves * chunks):
        a, c = i // chunks, i % chunks
        loads[1 + i].wait()
        stage[a, c] = dot(hid[a], roll[a, c]).astype(jnp.bfloat16)
        stores.append(
            pltpu.make_async_copy(stage.at[a, c], prop_o.at[:, pl.ds(i * width, width)], store_sem.at[i])
        )
        stores[-1].start()
    for copy in loads[1 + halves * chunks :]:
        copy.wait()
    fresh = adam(opt[0], opt[1], opt[2], opt[3])
    for i, ref in enumerate((mom_o, sec_o, mas_o)):
        opt_new[i] = fresh[i]
        stores.append(pltpu.make_async_copy(opt_new.at[i], ref, store_sem.at[halves * chunks + i]))
        stores[-1].start()
    for copy in stores:
        copy.wait()


def local(
    acts,
    out_grad,
    moment,
    second,
    master,
    queries,
    cache_keys,
    cache_values,
    tree_keys,
    tree_values,
    parents,
    lengths,
    residual,
    out_proj,
    *,
    grid,
    nt,
):
    nx, ny, nz = grid
    chunks = 2
    rows = acts.shape[1]
    columns = out_grad.shape[1]
    width = columns // (2 * chunks)
    tiles = width // LANES * chunks
    pad = -(-tiles // 16) * 16
    nodes, heads, depth = queries.shape[1:]
    cache = cache_keys.shape[1]
    side = ny * nz
    bf16, f32 = jnp.bfloat16, jnp.float32
    hbm = pl.BlockSpec(memory_space=pltpu.HBM)
    dma = pltpu.SemaphoreType.DMA
    limit = 56 * 1024 * 1024
    g_row, hidden, roll = pl.pallas_call(
        functools.partial(step_kernel, (nx, ny, nz, nt, chunks)),
        out_shape=[
            jax.ShapeDtypeStruct((1, columns), f32),
            jax.ShapeDtypeStruct((2, nodes, rows), bf16),
            jax.ShapeDtypeStruct((2, chunks, rows, width), bf16),
        ],
        in_specs=[hbm] * 14,
        out_specs=[hbm] * 3,
        scratch_shapes=[
            pltpu.VMEM(acts.shape, bf16),
            pltpu.VMEM((2, chunks, acts.shape[0], width), bf16),
            pltpu.VMEM((3, 1, columns), f32),
            pltpu.VMEM((3, 2, tiles, LANES), f32),
            pltpu.VMEM((nodes * heads, depth), bf16),
            pltpu.VMEM((cache, depth), bf16),
            pltpu.VMEM((cache, depth), bf16),
            pltpu.VMEM((nodes, depth), bf16),
            pltpu.VMEM((nodes, depth), bf16),
            pltpu.VMEM((1, nodes), jnp.int32),
            pltpu.VMEM((1, 1), jnp.int32),
            pltpu.VMEM((nodes, rows), bf16),
            pltpu.VMEM(out_proj.shape, bf16),
            pltpu.VMEM((2, chunks, rows, width), f32),
            pltpu.VMEM((2, chunks, rows, width), bf16),
            pltpu.VMEM((2, chunks, nx - 1, side, width), bf16),
            pltpu.VMEM((2, side * pad, LANES), f32),
            pltpu.VMEM((2, side, pad, LANES), bf16),
            pltpu.VMEM((2, side - 1, pad, LANES), bf16),
            pltpu.VMEM((2, side, pad, LANES), bf16),
            pltpu.VMEM((2, chunks, side, width), bf16),
            pltpu.VMEM((nodes * heads, depth), f32),
            pltpu.VMEM((nodes, rows), f32),
            pltpu.VMEM((nt - 1, nodes // nt, rows), f32),
            pltpu.VMEM((nodes, rows), f32),
            pltpu.VMEM((2, nodes, rows), bf16),
            pltpu.VMEM((1, columns), f32),
            pltpu.VMEM((2, pad, LANES), f32),
            dma((13 + 2 * chunks,)),
            dma((2 + 2 * chunks,)),
            dma((2, chunks)),
            dma((2, chunks)),
            dma((2,)),
            dma((2,)),
            dma((2,)),
            dma((2,)),
            dma((2, chunks)),
            dma((2, chunks)),
            dma((2,)),
            dma((2,)),
        ],
        compiler_params=pltpu.CompilerParams(
            collective_id=0, has_side_effects=True, vmem_limit_bytes=limit
        ),
    )(
        acts,
        out_grad,
        moment,
        second,
        master,
        queries.reshape(nodes * heads, depth),
        cache_keys.reshape(cache, depth),
        cache_values.reshape(cache, depth),
        tree_keys.reshape(nodes, depth),
        tree_values.reshape(nodes, depth),
        parents,
        lengths.reshape(1, 1),
        residual.reshape(nodes, rows),
        out_proj,
    )
    moment_new, second_new, master_new, proposal = pl.pallas_call(
        result_kernel,
        out_shape=[jax.ShapeDtypeStruct(moment.shape, f32)] * 3
        + [jax.ShapeDtypeStruct((nodes, columns), bf16)],
        in_specs=[hbm] * 6,
        out_specs=[hbm] * 4,
        scratch_shapes=[
            pltpu.VMEM((2, chunks, rows, width), bf16),
            pltpu.VMEM((2, nodes, rows), bf16),
            pltpu.VMEM((4, 1, columns), f32),
            pltpu.VMEM((3, 1, columns), f32),
            pltpu.VMEM((2, chunks, nodes, width), bf16),
            dma((5 + 2 * chunks,)),
            dma((3 + 2 * chunks,)),
        ],
        compiler_params=pltpu.CompilerParams(vmem_limit_bytes=limit),
    )(roll, hidden, g_row, moment, second, master)
    return (moment_new, second_new, master_new, proposal.reshape(1, nodes, columns))


def solution(mesh):
    in_specs = (
        P("fsdp", None),
        P("fsdp", "tp"),
        P("fsdp", "tp"),
        P("fsdp", "tp"),
        P("fsdp", "tp"),
        P("fsdp", None, "tp", None),
        P("fsdp", None, "tp", None),
        P("fsdp", None, "tp", None),
        P("fsdp", None, "tp", None),
        P("fsdp", None, "tp", None),
        P("fsdp", None),
        P("fsdp"),
        P("fsdp", None, None),
        P("tp", None),
    )
    out_specs = (P("fsdp", "tp"), P("fsdp", "tp"), P("fsdp", "tp"), P("fsdp", None, "tp"))
    body = functools.partial(local, grid=GRIDS[mesh.shape["fsdp"]], nt=mesh.shape["tp"])
    return jax.shard_map(body, mesh=mesh, in_specs=in_specs, out_specs=out_specs, check_vma=False)
```

```python
import functools

import jax
import jax.numpy as jnp
from jax import lax
from jax.experimental import pallas as pl
from jax.experimental.pallas import tpu as pltpu
from jax.sharding import PartitionSpec as P

beta_one = 0.9
beta_two = 0.95
adam_eps = 1e-08
learn_rate = 0.001
weight_decay = 0.1
adam_count = 10
masked_score = -1e30

MESH = pl.DeviceIdType.MESH
LANES = 128
GRIDS = {128: (8, 8, 2), 32: (4, 4, 2), 16: (4, 4, 1), 8: (2, 2, 2)}


def nt_dot(a, b):
    return lax.dot_general(a, b, (((1,), (1,)), ((), ())), preferred_element_type=jnp.float32)


def dot(a, b):
    return jnp.dot(a, b, preferred_element_type=jnp.float32)


def adam(g, moment, second, master):
    moment_new = beta_one * moment + (1.0 - beta_one) * g
    second_new = beta_two * second + (1.0 - beta_two) * g * g
    corr_one = 1.0 - beta_one**adam_count
    corr_two = 1.0 - beta_two**adam_count
    direction = moment_new / corr_one / (jnp.sqrt(second_new / corr_two) + adam_eps)
    master_new = master - learn_rate * (direction + weight_decay * master)
    return moment_new, second_new, master_new


def step_kernel(
    cfg,
    acts_h,
    og_h,
    mom_h,
    sec_h,
    mas_h,
    q_h,
    k_h,
    v_h,
    tk_h,
    tv_h,
    par_h,
    len_h,
    res_h,
    op_h,
    g_o,
    hid_o,
    roll_o,
    acts,
    og,
    opt,
    opt_t,
    q,
    k,
    v,
    tk,
    tv,
    par,
    length,
    res,
    op,
    grad,
    rs_out,
    rs_in,
    tile_f,
    tile_out,
    tile_in,
    row_all,
    blk,
    qf,
    ht,
    ht_in,
    hid,
    g_row,
    own,
    load_sem,
    store_sem,
    rs_send,
    rs_recv,
    ex_send,
    ex_recv,
    row_send,
    row_recv,
    ag_send,
    ag_recv,
    tp_send,
    tp_recv,
):
    nx, ny, nz, nt, chunks = cfg
    rows = acts.shape[1]
    width = grad.shape[-1]
    per = width // LANES
    tiles = per * chunks
    pad = tile_out.shape[2]
    nodes = res.shape[0]
    heads = q.shape[0] // nodes
    legs = nt.bit_length() - 1

    f = lax.axis_index("fsdp")
    t = lax.axis_index("tp")
    x, y, z = f // (ny * nz), lax.rem(f // nz, ny), lax.rem(f, nz)
    sides = (nx, ny)
    pos = (x, y)
    group = (ny * nz, nx * nz)
    mine = (y * nz + z, x * nz + z)

    def line_peer(a, at):
        if a == 0:
            return (at * ny + y) * nz + z
        return (x * ny + at) * nz + z

    def group_peer(a, j):
        if a == 0:
            return x * (ny * nz) + j
        return ((j // nz) * ny + y) * nz + lax.rem(j, nz)

    def across(leg):
        step = 1 << leg
        return t + step - 2 * step * lax.rem(t // step, 2)

    def far_first(n):
        return sorted(range(1, n), key=lambda kk: -min(kk, n - kk))

    loads = {}

    def load(name, src, dst):
        copy = pltpu.make_async_copy(src, dst, load_sem.at[len(loads)])
        copy.start()
        loads[name] = copy

    load("acts", acts_h, acts)
    for c in range(chunks):
        for a in range(2):
            base = (a * chunks + c) * width
            load(("og", a, c), og_h.at[:, pl.ds(base, width)], og.at[a, c])

    barrier = pltpu.get_barrier_semaphore()
    count = 0
    for a in range(2):
        for kk in far_first(sides[a]):
            peer = line_peer(a, lax.rem(pos[a] + kk, sides[a]))
            pl.semaphore_signal(barrier, inc=1, device_id=(peer, t), device_id_type=MESH)
            count += 1
    for zz in range(1, nz):
        peer = (x * ny + y) * nz + lax.rem(z + zz, nz)
        pl.semaphore_signal(barrier, inc=1, device_id=(peer, t), device_id_type=MESH)
        count += 1
    for leg in range(legs):
        pl.semaphore_signal(barrier, inc=1, device_id=(f, across(leg)), device_id_type=MESH)
        count += 1

    row_at = lax.broadcasted_iota(jnp.int32, (rows, rows), 0)
    col_at = lax.broadcasted_iota(jnp.int32, (rows, rows), 1)
    py, px, pz = row_at // (nx * nz), lax.rem(row_at // nz, nx), lax.rem(row_at, nz)
    swap = (col_at == (px * ny + py) * nz + pz).astype(jnp.bfloat16)
    same = (col_at == row_at).astype(jnp.bfloat16)
    loads["acts"].wait()
    acts_t = [nt_dot(m, acts[...]).astype(jnp.bfloat16) for m in (same, swap)]

    def block(a, at):
        depth = rows // sides[a]
        return pl.ds(pl.multiple_of(at * depth, depth), depth)

    def wait_for(ref, sem):
        pltpu.make_async_copy(ref, ref, sem).wait()

    for c in range(chunks):
        for a in range(2):
            n = sides[a]
            loads[("og", a, c)].wait()
            value = dot(acts_t[a], og[a, c])
            grad[a, c] = value
            rs_out[a, c] = value.astype(jnp.bfloat16)
            if c == 0 and a == 0:
                pl.semaphore_wait(barrier, count)
            for kk in far_first(n):
                at = lax.rem(pos[a] + kk, n)
                pltpu.make_async_remote_copy(
                    src_ref=rs_out.at[a, c, block(a, at)],
                    dst_ref=rs_in.at[a, c, kk - 1],
                    send_sem=rs_send.at[a, c],
                    recv_sem=rs_recv.at[a, c],
                    device_id=(line_peer(a, at), t),
                    device_id_type=MESH,
                ).start()

    load("par", par_h, par)
    load("q", q_h, q)
    load("tk", tk_h, tk)
    load("k", k_h, k)
    load("len", len_h, length)
    load("v", v_h, v)
    load("tv", tv_h, tv)
    load("op", op_h, op)
    load("mom", mom_h, opt.at[0])
    load("sec", sec_h, opt.at[1])
    load("mas", mas_h, opt.at[2])
    load("res", res_h, res)
    tile_f[...] = jnp.zeros_like(tile_f)

    loads["par"].wait()
    j_at = lax.broadcasted_iota(jnp.int32, (nodes, nodes), 0)
    i_at = lax.broadcasted_iota(jnp.int32, (nodes, nodes), 1)
    links = ((par[...] == j_at) & (i_at > 0)) | (i_at == j_at)
    reach = links.astype(jnp.bfloat16)
    for _ in range(max(1, (nodes - 1).bit_length())):
        reach = jnp.minimum(dot(reach, reach), 1.0).astype(jnp.bfloat16)
    pick_row = lax.broadcasted_iota(jnp.int32, (2 * nodes, nodes), 0)
    pick_col = lax.broadcasted_iota(jnp.int32, (2 * nodes, nodes), 1)
    pick = (lax.rem(pick_row, nodes) == pick_col).astype(jnp.bfloat16)
    admitted = nt_dot(pick, reach) > 0.5
    loads["q"].wait()
    qf[...] = q[...].astype(jnp.float32)

    depth = q.shape[1]
    scale = depth ** (-0.5)
    for name in ("tk", "k", "len", "v", "tv", "op"):
        loads[name].wait()

    def attend(u):
        pair = jnp.concatenate(
            [qf[pl.ds(2 * u + e, nodes, stride=heads), :] for e in range(2)], axis=0
        ).astype(jnp.bfloat16)
        s_cache = nt_dot(pair, k[...])
        s_tree = nt_dot(pair, tk[...])
        live = lax.broadcasted_iota(jnp.int32, s_cache.shape, 1) < length[...]
        s_cache = jnp.where(live, s_cache, masked_score)
        s_tree = jnp.where(admitted, s_tree, masked_score)
        top = jnp.maximum(
            jnp.max(s_cache, axis=1, keepdims=True), jnp.max(s_tree, axis=1, keepdims=True)
        )
        e_cache = jnp.exp((s_cache - top) * scale)
        e_tree = jnp.exp((s_tree - top) * scale)
        total = jnp.sum(e_cache, axis=1, keepdims=True) + jnp.sum(e_tree, axis=1, keepdims=True)
        mixed = dot(e_cache.astype(jnp.bfloat16), v[...]) + dot(e_tree.astype(jnp.bfloat16), tv[...])
        mixed = (mixed / total).astype(jnp.bfloat16)
        add = dot(mixed[:nodes], op[pl.ds(2 * u * depth, depth), :]) + dot(
            mixed[nodes:], op[pl.ds((2 * u + 1) * depth, depth), :]
        )
        if u == 0:
            ht[0] = add
        else:
            ht[0] += add

    units = heads // 2
    early = units - 1
    for u in range(early):
        attend(u)

    for i, name in enumerate(("mom", "sec", "mas")):
        loads[name].wait()
        for a in range(2):
            for e in range(tiles):
                opt_t[i, a, pl.ds(e, 1), :] = opt[i, :, pl.ds((a * tiles + e) * LANES, LANES)]
    loads["res"].wait()

    wait_for(rs_in.at[1, 0], rs_recv.at[1, 0])
    for a in range(2):
        n = sides[a]
        for c in range(chunks):
            if (a, c) != (1, 0):
                wait_for(rs_in.at[a, c], rs_recv.at[a, c])
            value = grad[a, c, block(a, pos[a]), :]
            for kk in range(n - 1):
                value = value + rs_in[a, c, kk].astype(jnp.float32)
            for e in range(per):
                tile_f[a, pl.ds(c * per + e, group[a], stride=pad), :] = value[:, e * LANES : (e + 1) * LANES]
        tile_out[a] = tile_f[a].astype(jnp.bfloat16).reshape(group[a], pad, LANES)
        for kk in far_first(group[a]):
            j = lax.rem(mine[a] + kk, group[a])
            pltpu.make_async_remote_copy(
                src_ref=tile_out.at[a, j],
                dst_ref=tile_in.at[a, kk - 1],
                send_sem=ex_send.at[a],
                recv_sem=ex_recv.at[a],
                device_id=(group_peer(a, j), t),
                device_id_type=MESH,
            ).start()
        own[a] = tile_f[a, pl.ds(pl.multiple_of(mine[a] * pad, pad), pad), :]

    for u in range(early, units):
        attend(u)

    leg_copies = []

    def leg_start(leg):
        copy = pltpu.make_async_remote_copy(
            src_ref=ht.at[leg],
            dst_ref=ht_in.at[leg],
            send_sem=tp_send.at[leg],
            recv_sem=tp_recv.at[leg],
            device_id=(f, across(leg)),
            device_id_type=MESH,
        )
        copy.start()
        leg_copies.append(copy)

    def leg_end(leg):
        leg_copies[leg].wait_recv()
        ht[leg + 1] = ht[leg] + ht_in[leg]
        if leg + 1 < legs:
            leg_start(leg + 1)

    leg_start(0)

    g_tiles = []
    for a in range(2):
        wait_for(tile_in.at[a], ex_recv.at[a])
        g = own[a]
        for kk in range(group[a] - 1):
            g = g + tile_in[a, kk].astype(jnp.float32)
        g = g[:tiles]
        g_tiles.append(g)
        master_new = adam(g, opt_t[0, a], opt_t[1, a], opt_t[2, a])[2]
        if pad > tiles:
            fill = jnp.zeros((pad - tiles, LANES), jnp.float32)
            master_new = jnp.concatenate([master_new, fill], axis=0)
        row_all[a, mine[a]] = master_new.astype(jnp.bfloat16)
        for kk in far_first(group[a]):
            j = lax.rem(mine[a] + kk, group[a])
            pltpu.make_async_remote_copy(
                src_ref=row_all.at[a, mine[a]],
                dst_ref=row_all.at[a, mine[a]],
                send_sem=row_send.at[a],
                recv_sem=row_recv.at[a],
                device_id=(group_peer(a, j), t),
                device_id_type=MESH,
            ).start()

    stores = []

    def store(src, dst):
        copy = pltpu.make_async_copy(src, dst, store_sem.at[len(stores)])
        copy.start()
        stores.append(copy)

    for a in range(2):
        for e in range(tiles):
            g_row[:, pl.ds((a * tiles + e) * LANES, LANES)] = g_tiles[a][e : e + 1]
    store(g_row, g_o)

    leg_end(0)

    for a in range(2):
        n = sides[a]
        wait_for(row_all.at[a, pl.ds(0, group[a] - 1)], row_recv.at[a])
        tile_f[a] = row_all[a].astype(jnp.float32).reshape(group[a] * pad, LANES)
        for c in range(chunks):
            for e in range(per):
                blk[a, c, :, pl.ds(e * LANES, LANES)] = tile_f[
                    a, pl.ds(c * per + e, group[a], stride=pad), :
                ].astype(jnp.bfloat16)
            for kk in far_first(n):
                at = lax.rem(pos[a] + kk, n)
                pltpu.make_async_remote_copy(
                    src_ref=blk.at[a, c],
                    dst_ref=roll_o.at[a, c, block(a, pos[a])],
                    send_sem=ag_send.at[a, c],
                    recv_sem=ag_recv.at[a, c],
                    device_id=(line_peer(a, at), t),
                    device_id_type=MESH,
                ).start()
            store(blk.at[a, c], roll_o.at[a, c, block(a, pos[a])])

    for leg in range(1, legs):
        leg_end(leg)
    hidden = (res[...].astype(jnp.float32) + ht[legs]).astype(jnp.bfloat16)
    hid[0] = hidden
    hid[1] = nt_dot(hidden, swap).astype(jnp.bfloat16)
    store(hid, hid_o)

    for a in range(2):
        for c in range(chunks):
            wait_for(rs_in.at[a, c], rs_send.at[a, c])
        wait_for(tile_in.at[a], ex_send.at[a])
        wait_for(row_all.at[a, pl.ds(0, group[a] - 1)], row_send.at[a])
    for copy in leg_copies:
        copy.wait_send()
    for a in range(2):
        n = sides[a]
        for c in range(chunks):
            others = pl.ds(0, rows - rows // n)
            wait_for(roll_o.at[a, c, others], ag_send.at[a, c])
            wait_for(roll_o.at[a, c, others], ag_recv.at[a, c])
    for copy in stores:
        copy.wait()


def result_kernel(
    roll_h, hid_h, g_h, mom_h, sec_h, mas_h, mom_o, sec_o, mas_o, prop_o, roll, hid, opt, opt_new, stage, load_sem, store_sem
):
    halves, chunks, _, width = roll.shape
    parts = halves * chunks
    pairs = [(ref, opt.at[i]) for i, ref in enumerate((g_h, mom_h, sec_h, mas_h))] + [(hid_h, hid)]
    for i in range(parts):
        at = (i // chunks, i % chunks)
        pairs.append((roll_h.at[at], roll.at[at]))
    loads = [pltpu.make_async_copy(src, dst, load_sem.at[i]) for i, (src, dst) in enumerate(pairs)]
    for copy in loads:
        copy.start()
    stores = []

    def store(src, dst):
        copy = pltpu.make_async_copy(src, dst, store_sem.at[len(stores)])
        copy.start()
        stores.append(copy)

    for copy in loads[:4]:
        copy.wait()
    fresh = adam(opt[0], opt[1], opt[2], opt[3])
    for i, ref in enumerate((mom_o, sec_o, mas_o)):
        opt_new[i] = fresh[i]
        store(opt_new.at[i], ref)
    loads[4].wait()
    for i in range(parts):
        a, c = i // chunks, i % chunks
        loads[5 + i].wait()
        stage[a, c] = dot(hid[a], roll[a, c]).astype(jnp.bfloat16)
        store(stage.at[a, c], prop_o.at[:, pl.ds(i * width, width)])
    for copy in stores:
        copy.wait()


def local(
    acts,
    out_grad,
    moment,
    second,
    master,
    queries,
    cache_keys,
    cache_values,
    tree_keys,
    tree_values,
    parents,
    lengths,
    residual,
    out_proj,
    *,
    grid,
    nt,
):
    nx, ny, nz = grid
    chunks = 2
    rows = acts.shape[1]
    columns = out_grad.shape[1]
    width = columns // (2 * chunks)
    tiles = width // LANES * chunks
    pad = -(-tiles // 16) * 16
    nodes, heads, depth = queries.shape[1:]
    cache = cache_keys.shape[1]
    side = ny * nz
    legs = nt.bit_length() - 1
    bf16, f32 = jnp.bfloat16, jnp.float32
    hbm = pl.BlockSpec(memory_space=pltpu.HBM)
    dma = pltpu.SemaphoreType.DMA
    limit = 56 * 1024 * 1024
    g_row, hidden, roll = pl.pallas_call(
        functools.partial(step_kernel, (nx, ny, nz, nt, chunks)),
        out_shape=[
            jax.ShapeDtypeStruct((1, columns), f32),
            jax.ShapeDtypeStruct((2, nodes, rows), bf16),
            jax.ShapeDtypeStruct((2, chunks, rows, width), bf16),
        ],
        in_specs=[hbm] * 14,
        out_specs=[hbm] * 3,
        scratch_shapes=[
            pltpu.VMEM(acts.shape, bf16),
            pltpu.VMEM((2, chunks, acts.shape[0], width), bf16),
            pltpu.VMEM((3, 1, columns), f32),
            pltpu.VMEM((3, 2, tiles, LANES), f32),
            pltpu.VMEM((nodes * heads, depth), bf16),
            pltpu.VMEM((cache, depth), bf16),
            pltpu.VMEM((cache, depth), bf16),
            pltpu.VMEM((nodes, depth), bf16),
            pltpu.VMEM((nodes, depth), bf16),
            pltpu.VMEM((1, nodes), jnp.int32),
            pltpu.VMEM((1, 1), jnp.int32),
            pltpu.VMEM((nodes, rows), bf16),
            pltpu.VMEM(out_proj.shape, bf16),
            pltpu.VMEM((2, chunks, rows, width), f32),
            pltpu.VMEM((2, chunks, rows, width), bf16),
            pltpu.VMEM((2, chunks, nx - 1, side, width), bf16),
            pltpu.VMEM((2, side * pad, LANES), f32),
            pltpu.VMEM((2, side, pad, LANES), bf16),
            pltpu.VMEM((2, side - 1, pad, LANES), bf16),
            pltpu.VMEM((2, side, pad, LANES), bf16),
            pltpu.VMEM((2, chunks, side, width), bf16),
            pltpu.VMEM((nodes * heads, depth), f32),
            pltpu.VMEM((legs + 1, nodes, rows), f32),
            pltpu.VMEM((legs, nodes, rows), f32),
            pltpu.VMEM((2, nodes, rows), bf16),
            pltpu.VMEM((1, columns), f32),
            pltpu.VMEM((2, pad, LANES), f32),
            dma((13 + 2 * chunks,)),
            dma((2 + 2 * chunks,)),
            dma((2, chunks)),
            dma((2, chunks)),
            dma((2,)),
            dma((2,)),
            dma((2,)),
            dma((2,)),
            dma((2, chunks)),
            dma((2, chunks)),
            dma((legs,)),
            dma((legs,)),
        ],
        compiler_params=pltpu.CompilerParams(
            collective_id=0, has_side_effects=True, vmem_limit_bytes=limit
        ),
    )(
        acts,
        out_grad,
        moment,
        second,
        master,
        queries.reshape(nodes * heads, depth),
        cache_keys.reshape(cache, depth),
        cache_values.reshape(cache, depth),
        tree_keys.reshape(nodes, depth),
        tree_values.reshape(nodes, depth),
        parents,
        lengths.reshape(1, 1),
        residual.reshape(nodes, rows),
        out_proj,
    )
    moment_new, second_new, master_new, proposal = pl.pallas_call(
        result_kernel,
        out_shape=[jax.ShapeDtypeStruct(moment.shape, f32)] * 3
        + [jax.ShapeDtypeStruct((nodes, columns), bf16)],
        in_specs=[hbm] * 6,
        out_specs=[hbm] * 4,
        scratch_shapes=[
            pltpu.VMEM((2, chunks, rows, width), bf16),
            pltpu.VMEM((2, nodes, rows), bf16),
            pltpu.VMEM((4, 1, columns), f32),
            pltpu.VMEM((3, 1, columns), f32),
            pltpu.VMEM((2, chunks, nodes, width), bf16),
            dma((5 + 2 * chunks,)),
            dma((3 + 2 * chunks,)),
        ],
        compiler_params=pltpu.CompilerParams(vmem_limit_bytes=limit),
    )(roll, hidden, g_row, moment, second, master)
    return (moment_new, second_new, master_new, proposal.reshape(1, nodes, columns))


def solution(mesh):
    in_specs = (
        P("fsdp", None),
        P("fsdp", "tp"),
        P("fsdp", "tp"),
        P("fsdp", "tp"),
        P("fsdp", "tp"),
        P("fsdp", None, "tp", None),
        P("fsdp", None, "tp", None),
        P("fsdp", None, "tp", None),
        P("fsdp", None, "tp", None),
        P("fsdp", None, "tp", None),
        P("fsdp", None),
        P("fsdp"),
        P("fsdp", None, None),
        P("tp", None),
    )
    out_specs = (P("fsdp", "tp"), P("fsdp", "tp"), P("fsdp", "tp"), P("fsdp", None, "tp"))
    body = functools.partial(local, grid=GRIDS[mesh.shape["fsdp"]], nt=mesh.shape["tp"])
    return jax.shard_map(body, mesh=mesh, in_specs=in_specs, out_specs=out_specs, check_vma=False)
```

```python
import functools

import jax
import jax.numpy as jnp
from jax import lax
from jax.experimental import pallas as pl
from jax.experimental.pallas import tpu as pltpu
from jax.sharding import PartitionSpec as P

beta_one = 0.9
beta_two = 0.95
adam_eps = 1e-08
learn_rate = 0.001
weight_decay = 0.1
adam_count = 10
masked_score = -1e30

MESH = pl.DeviceIdType.MESH
LANES = 128
GRIDS = {128: (8, 8, 2)}


def nt_dot(a, b):
    return lax.dot_general(a, b, (((1,), (1,)), ((), ())), preferred_element_type=jnp.float32)


def dot(a, b):
    return jnp.dot(a, b, preferred_element_type=jnp.float32)


def adam(g, moment, second, master):
    moment_new = beta_one * moment + (1.0 - beta_one) * g
    second_new = beta_two * second + (1.0 - beta_two) * g * g
    corr_one = 1.0 - beta_one**adam_count
    corr_two = 1.0 - beta_two**adam_count
    direction = moment_new / corr_one / (jnp.sqrt(second_new / corr_two) + adam_eps)
    master_new = master - learn_rate * (direction + weight_decay * master)
    return moment_new, second_new, master_new


def step_kernel(
    cfg,
    acts_h,
    og_h,
    mom_h,
    sec_h,
    mas_h,
    q_h,
    k_h,
    v_h,
    tk_h,
    tv_h,
    par_h,
    len_h,
    res_h,
    op_h,
    g_o,
    hid_o,
    roll_o,
    acts,
    og,
    opt,
    opt_t,
    q,
    k,
    v,
    tk,
    tv,
    par,
    length,
    res,
    op,
    grad,
    rs_out,
    rs_in,
    tile_f,
    tile_out,
    tile_in,
    row_all,
    blk,
    relay,
    qf,
    ht,
    ht_in,
    hid,
    g_row,
    own,
    load_sem,
    store_sem,
    rs_send,
    rs_recv,
    ex_send,
    ex_recv,
    row_send,
    row_recv,
    ag_send,
    ag_recv,
    tp_send,
    tp_recv,
):
    nx, ny, nz, nt, chunks = cfg
    rows = acts.shape[1]
    width = grad.shape[-1]
    per = width // LANES
    tiles = per * chunks
    pad = tile_out.shape[2]
    nodes = res.shape[0]
    heads = q.shape[0] // nodes
    legs = nt.bit_length() - 1

    f = lax.axis_index("fsdp")
    t = lax.axis_index("tp")
    x, y, z = f // (ny * nz), lax.rem(f // nz, ny), lax.rem(f, nz)
    sides = (nx, ny)
    pos = (x, y)
    group = (ny * nz, nx * nz)
    mine = (y * nz + z, x * nz + z)

    def line_peer(a, at):
        if a == 0:
            return (at * ny + y) * nz + z
        return (x * ny + at) * nz + z

    def group_peer(a, j):
        if a == 0:
            return x * (ny * nz) + j
        return ((j // nz) * ny + y) * nz + lax.rem(j, nz)

    def across(leg):
        step = 1 << leg
        return t + step - 2 * step * lax.rem(t // step, 2)

    def far_first(n):
        return sorted(range(1, n), key=lambda kk: -min(kk, n - kk))

    loads = {}

    def load(name, src, dst):
        copy = pltpu.make_async_copy(src, dst, load_sem.at[len(loads)])
        copy.start()
        loads[name] = copy

    load("acts", acts_h, acts)
    for c in range(chunks):
        for a in range(2):
            base = (a * chunks + c) * width
            load(("og", a, c), og_h.at[:, pl.ds(base, width)], og.at[a, c])

    barrier = pltpu.get_barrier_semaphore()
    count = 0
    for a in range(2):
        for kk in far_first(sides[a]):
            peer = line_peer(a, lax.rem(pos[a] + kk, sides[a]))
            pl.semaphore_signal(barrier, inc=1, device_id=(peer, t), device_id_type=MESH)
            count += 1
    for zz in range(1, nz):
        peer = (x * ny + y) * nz + lax.rem(z + zz, nz)
        pl.semaphore_signal(barrier, inc=1, device_id=(peer, t), device_id_type=MESH)
        count += 1
    for leg in range(legs):
        pl.semaphore_signal(barrier, inc=1, device_id=(f, across(leg)), device_id_type=MESH)
        count += 1

    row_at = lax.broadcasted_iota(jnp.int32, (rows, rows), 0)
    col_at = lax.broadcasted_iota(jnp.int32, (rows, rows), 1)
    py, px, pz = row_at // (nx * nz), lax.rem(row_at // nz, nx), lax.rem(row_at, nz)
    swap = (col_at == (px * ny + py) * nz + pz).astype(jnp.bfloat16)
    same = (col_at == row_at).astype(jnp.bfloat16)
    loads["acts"].wait()
    acts_t = [nt_dot(m, acts[...]).astype(jnp.bfloat16) for m in (same, swap)]

    def block(a, at):
        depth = rows // sides[a]
        return pl.ds(pl.multiple_of(at * depth, depth), depth)

    def wait_for(ref, sem):
        pltpu.make_async_copy(ref, ref, sem).wait()

    for c in range(chunks):
        for a in range(2):
            n = sides[a]
            loads[("og", a, c)].wait()
            value = dot(acts_t[a], og[a, c])
            grad[a, c] = value
            rs_out[a, c] = value.astype(jnp.bfloat16)
            if c == 0 and a == 0:
                pl.semaphore_wait(barrier, count)
            for kk in far_first(n):
                at = lax.rem(pos[a] + kk, n)
                pltpu.make_async_remote_copy(
                    src_ref=rs_out.at[a, c, block(a, at)],
                    dst_ref=rs_in.at[a, c, kk - 1],
                    send_sem=rs_send.at[a, c],
                    recv_sem=rs_recv.at[a, c],
                    device_id=(line_peer(a, at), t),
                    device_id_type=MESH,
                ).start()

    load("par", par_h, par)
    load("q", q_h, q)
    load("tk", tk_h, tk)
    load("k", k_h, k)
    load("len", len_h, length)
    load("v", v_h, v)
    load("tv", tv_h, tv)
    load("op", op_h, op)
    load("mom", mom_h, opt.at[0])
    load("sec", sec_h, opt.at[1])
    load("mas", mas_h, opt.at[2])
    load("res", res_h, res)
    tile_f[...] = jnp.zeros_like(tile_f)

    loads["par"].wait()
    j_at = lax.broadcasted_iota(jnp.int32, (nodes, nodes), 0)
    i_at = lax.broadcasted_iota(jnp.int32, (nodes, nodes), 1)
    links = ((par[...] == j_at) & (i_at > 0)) | (i_at == j_at)
    reach = links.astype(jnp.bfloat16)
    for _ in range(max(1, (nodes - 1).bit_length())):
        reach = jnp.minimum(dot(reach, reach), 1.0).astype(jnp.bfloat16)
    pick_row = lax.broadcasted_iota(jnp.int32, (2 * nodes, nodes), 0)
    pick_col = lax.broadcasted_iota(jnp.int32, (2 * nodes, nodes), 1)
    pick = (lax.rem(pick_row, nodes) == pick_col).astype(jnp.bfloat16)
    admitted = nt_dot(pick, reach) > 0.5
    loads["q"].wait()
    qf[...] = q[...].astype(jnp.float32)

    depth = q.shape[1]
    scale = depth ** (-0.5)
    for name in ("tk", "k", "len", "v", "tv", "op"):
        loads[name].wait()

    def attend(u):
        pair = jnp.concatenate(
            [qf[pl.ds(2 * u + e, nodes, stride=heads), :] for e in range(2)], axis=0
        ).astype(jnp.bfloat16)
        s_cache = nt_dot(pair, k[...])
        s_tree = nt_dot(pair, tk[...])
        live = lax.broadcasted_iota(jnp.int32, s_cache.shape, 1) < length[...]
        s_cache = jnp.where(live, s_cache, masked_score)
        s_tree = jnp.where(admitted, s_tree, masked_score)
        top = jnp.maximum(
            jnp.max(s_cache, axis=1, keepdims=True), jnp.max(s_tree, axis=1, keepdims=True)
        )
        e_cache = jnp.exp((s_cache - top) * scale)
        e_tree = jnp.exp((s_tree - top) * scale)
        total = jnp.sum(e_cache, axis=1, keepdims=True) + jnp.sum(e_tree, axis=1, keepdims=True)
        mixed = dot(e_cache.astype(jnp.bfloat16), v[...]) + dot(e_tree.astype(jnp.bfloat16), tv[...])
        mixed = (mixed / total).astype(jnp.bfloat16)
        add = dot(mixed[:nodes], op[pl.ds(2 * u * depth, depth), :]) + dot(
            mixed[nodes:], op[pl.ds((2 * u + 1) * depth, depth), :]
        )
        if u == 0:
            ht[0] = add
        else:
            ht[0] += add

    units = heads // 2
    early = units - 1
    for u in range(early):
        attend(u)

    for i, name in enumerate(("mom", "sec", "mas")):
        loads[name].wait()
        for a in range(2):
            for e in range(tiles):
                opt_t[i, a, pl.ds(e, 1), :] = opt[i, :, pl.ds((a * tiles + e) * LANES, LANES)]
    loads["res"].wait()

    wait_for(rs_in.at[1, 0], rs_recv.at[1, 0])
    for a in range(2):
        n = sides[a]
        for c in range(chunks):
            if (a, c) != (1, 0):
                wait_for(rs_in.at[a, c], rs_recv.at[a, c])
            value = grad[a, c, block(a, pos[a]), :]
            for kk in range(n - 1):
                value = value + rs_in[a, c, kk].astype(jnp.float32)
            for e in range(per):
                tile_f[a, pl.ds(c * per + e, group[a], stride=pad), :] = value[:, e * LANES : (e + 1) * LANES]
        tile_out[a] = tile_f[a].astype(jnp.bfloat16).reshape(group[a], pad, LANES)
        for kk in far_first(group[a]):
            j = lax.rem(mine[a] + kk, group[a])
            pltpu.make_async_remote_copy(
                src_ref=tile_out.at[a, j],
                dst_ref=tile_in.at[a, kk - 1],
                send_sem=ex_send.at[a],
                recv_sem=ex_recv.at[a],
                device_id=(group_peer(a, j), t),
                device_id_type=MESH,
            ).start()
        own[a] = tile_f[a, pl.ds(pl.multiple_of(mine[a] * pad, pad), pad), :]

    for u in range(early, units):
        attend(u)

    leg_copies = []

    def leg_start(leg):
        copy = pltpu.make_async_remote_copy(
            src_ref=ht.at[leg],
            dst_ref=ht_in.at[leg],
            send_sem=tp_send.at[leg],
            recv_sem=tp_recv.at[leg],
            device_id=(f, across(leg)),
            device_id_type=MESH,
        )
        copy.start()
        leg_copies.append(copy)

    def leg_end(leg):
        leg_copies[leg].wait_recv()
        ht[leg + 1] = ht[leg] + ht_in[leg]
        if leg + 1 < legs:
            leg_start(leg + 1)

    leg_start(0)

    g_tiles = []
    for a in range(2):
        wait_for(tile_in.at[a], ex_recv.at[a])
        g = own[a]
        for kk in range(group[a] - 1):
            g = g + tile_in[a, kk].astype(jnp.float32)
        g = g[:tiles]
        g_tiles.append(g)
        master_new = adam(g, opt_t[0, a], opt_t[1, a], opt_t[2, a])[2]
        if pad > tiles:
            fill = jnp.zeros((pad - tiles, LANES), jnp.float32)
            master_new = jnp.concatenate([master_new, fill], axis=0)
        row_all[a, mine[a]] = master_new.astype(jnp.bfloat16)
        for kk in far_first(group[a]):
            j = lax.rem(mine[a] + kk, group[a])
            pltpu.make_async_remote_copy(
                src_ref=row_all.at[a, mine[a]],
                dst_ref=row_all.at[a, mine[a]],
                send_sem=row_send.at[a],
                recv_sem=row_recv.at[a],
                device_id=(group_peer(a, j), t),
                device_id_type=MESH,
            ).start()

    stores = []

    def store(src, dst):
        copy = pltpu.make_async_copy(src, dst, store_sem.at[len(stores)])
        copy.start()
        stores.append(copy)

    for a in range(2):
        for e in range(tiles):
            g_row[:, pl.ds((a * tiles + e) * LANES, LANES)] = g_tiles[a][e : e + 1]
    store(g_row, g_o)

    leg_end(0)

    ag_copies = []

    def ag_copy(a, c, d, kind, src, owner, step):
        n = sides[a]
        at = lax.rem(pos[a] + (1 - 2 * d) * step + n, n)
        landing = relay.at[a, c, d] if kind == 1 else roll_o.at[a, c, block(a, owner)]
        return pltpu.make_async_remote_copy(
            src_ref=src,
            dst_ref=landing,
            send_sem=ag_send.at[a, c, d, kind],
            recv_sem=ag_recv.at[a, c, d, kind],
            device_id=(line_peer(a, at), t),
            device_id_type=MESH,
        )

    def ag_start(*which):
        copy = ag_copy(*which)
        copy.start()
        ag_copies.append(copy)

    for a in range(2):
        wait_for(row_all.at[a, pl.ds(0, group[a] - 1)], row_recv.at[a])
        tile_f[a] = row_all[a].astype(jnp.float32).reshape(group[a] * pad, LANES)
        for c in range(chunks):
            for e in range(per):
                blk[a, c, :, pl.ds(e * LANES, LANES)] = tile_f[
                    a, pl.ds(c * per + e, group[a], stride=pad), :
                ].astype(jnp.bfloat16)
            for d in range(2):
                ag_start(a, c, d, 1, blk.at[a, c], pos[a], 2)
        for c in range(chunks):
            for d in range(2):
                ag_start(a, c, d, 0, blk.at[a, c], pos[a], 1)
            store(blk.at[a, c], roll_o.at[a, c, block(a, pos[a])])
    if legs > 1:
        leg_end(1)
    for a in range(2):
        n = sides[a]
        for c in range(chunks):
            for d in range(2):
                owner = lax.rem(pos[a] - 2 * (1 - 2 * d) + n, n)
                ag_copy(a, c, d, 1, blk.at[a, c], pos[a], 2).wait_recv()
                ag_start(a, c, d, 2, relay.at[a, c, d], owner, 1)
                if c % 2 == d:
                    ag_start(a, c, d, 3, relay.at[a, c, d], owner, 2)
                store(relay.at[a, c, d], roll_o.at[a, c, block(a, owner)])

    for leg in range(2, legs):
        leg_end(leg)
    hidden = (res[...].astype(jnp.float32) + ht[legs]).astype(jnp.bfloat16)
    hid[0] = hidden
    hid[1] = nt_dot(hidden, swap).astype(jnp.bfloat16)
    store(hid, hid_o)

    for a in range(2):
        for c in range(chunks):
            wait_for(rs_in.at[a, c], rs_send.at[a, c])
        wait_for(tile_in.at[a], ex_send.at[a])
        wait_for(row_all.at[a, pl.ds(0, group[a] - 1)], row_send.at[a])
    for copy in leg_copies:
        copy.wait_send()
    for copy in ag_copies:
        copy.wait_send()
    for a in range(2):
        for c in range(chunks):
            for d in range(2):
                for kind in (0, 2, 3):
                    if kind < 3 or c % 2 == d:
                        ag_copy(a, c, d, kind, blk.at[a, c], pos[a], 1).wait_recv()
    for copy in stores:
        copy.wait()


def result_kernel(
    roll_h, hid_h, g_h, mom_h, sec_h, mas_h, mom_o, sec_o, mas_o, prop_o, roll, hid, opt, opt_new, stage, load_sem, store_sem
):
    halves, chunks, _, width = roll.shape
    parts = halves * chunks
    pairs = [(ref, opt.at[i]) for i, ref in enumerate((g_h, mom_h, sec_h, mas_h))] + [(hid_h, hid)]
    for i in range(parts):
        at = (i // chunks, i % chunks)
        pairs.append((roll_h.at[at], roll.at[at]))
    loads = [pltpu.make_async_copy(src, dst, load_sem.at[i]) for i, (src, dst) in enumerate(pairs)]
    for copy in loads:
        copy.start()
    stores = []

    def store(src, dst):
        copy = pltpu.make_async_copy(src, dst, store_sem.at[len(stores)])
        copy.start()
        stores.append(copy)

    for copy in loads[:4]:
        copy.wait()
    fresh = adam(opt[0], opt[1], opt[2], opt[3])
    for i, ref in enumerate((mom_o, sec_o, mas_o)):
        opt_new[i] = fresh[i]
        store(opt_new.at[i], ref)
    loads[4].wait()
    for i in range(parts):
        a, c = i // chunks, i % chunks
        loads[5 + i].wait()
        stage[a, c] = dot(hid[a], roll[a, c]).astype(jnp.bfloat16)
        store(stage.at[a, c], prop_o.at[:, pl.ds(i * width, width)])
    for copy in stores:
        copy.wait()


def local(
    acts,
    out_grad,
    moment,
    second,
    master,
    queries,
    cache_keys,
    cache_values,
    tree_keys,
    tree_values,
    parents,
    lengths,
    residual,
    out_proj,
    *,
    grid,
    nt,
):
    nx, ny, nz = grid
    chunks = 2
    rows = acts.shape[1]
    columns = out_grad.shape[1]
    width = columns // (2 * chunks)
    tiles = width // LANES * chunks
    pad = -(-tiles // 16) * 16
    nodes, heads, depth = queries.shape[1:]
    cache = cache_keys.shape[1]
    side = ny * nz
    legs = nt.bit_length() - 1
    bf16, f32 = jnp.bfloat16, jnp.float32
    hbm = pl.BlockSpec(memory_space=pltpu.HBM)
    dma = pltpu.SemaphoreType.DMA
    limit = 56 * 1024 * 1024
    g_row, hidden, roll = pl.pallas_call(
        functools.partial(step_kernel, (nx, ny, nz, nt, chunks)),
        out_shape=[
            jax.ShapeDtypeStruct((1, columns), f32),
            jax.ShapeDtypeStruct((2, nodes, rows), bf16),
            jax.ShapeDtypeStruct((2, chunks, rows, width), bf16),
        ],
        in_specs=[hbm] * 14,
        out_specs=[hbm] * 3,
        scratch_shapes=[
            pltpu.VMEM(acts.shape, bf16),
            pltpu.VMEM((2, chunks, acts.shape[0], width), bf16),
            pltpu.VMEM((3, 1, columns), f32),
            pltpu.VMEM((3, 2, tiles, LANES), f32),
            pltpu.VMEM((nodes * heads, depth), bf16),
            pltpu.VMEM((cache, depth), bf16),
            pltpu.VMEM((cache, depth), bf16),
            pltpu.VMEM((nodes, depth), bf16),
            pltpu.VMEM((nodes, depth), bf16),
            pltpu.VMEM((1, nodes), jnp.int32),
            pltpu.VMEM((1, 1), jnp.int32),
            pltpu.VMEM((nodes, rows), bf16),
            pltpu.VMEM(out_proj.shape, bf16),
            pltpu.VMEM((2, chunks, rows, width), f32),
            pltpu.VMEM((2, chunks, rows, width), bf16),
            pltpu.VMEM((2, chunks, nx - 1, side, width), bf16),
            pltpu.VMEM((2, side * pad, LANES), f32),
            pltpu.VMEM((2, side, pad, LANES), bf16),
            pltpu.VMEM((2, side - 1, pad, LANES), bf16),
            pltpu.VMEM((2, side, pad, LANES), bf16),
            pltpu.VMEM((2, chunks, side, width), bf16),
            pltpu.VMEM((2, chunks, 2, side, width), bf16),
            pltpu.VMEM((nodes * heads, depth), f32),
            pltpu.VMEM((legs + 1, nodes, rows), f32),
            pltpu.VMEM((legs, nodes, rows), f32),
            pltpu.VMEM((2, nodes, rows), bf16),
            pltpu.VMEM((1, columns), f32),
            pltpu.VMEM((2, pad, LANES), f32),
            dma((13 + 2 * chunks,)),
            dma((2 + 6 * chunks,)),
            dma((2, chunks)),
            dma((2, chunks)),
            dma((2,)),
            dma((2,)),
            dma((2,)),
            dma((2,)),
            dma((2, chunks, 2, 4)),
            dma((2, chunks, 2, 4)),
            dma((legs,)),
            dma((legs,)),
        ],
        compiler_params=pltpu.CompilerParams(
            collective_id=0, has_side_effects=True, vmem_limit_bytes=limit
        ),
    )(
        acts,
        out_grad,
        moment,
        second,
        master,
        queries.reshape(nodes * heads, depth),
        cache_keys.reshape(cache, depth),
        cache_values.reshape(cache, depth),
        tree_keys.reshape(nodes, depth),
        tree_values.reshape(nodes, depth),
        parents,
        lengths.reshape(1, 1),
        residual.reshape(nodes, rows),
        out_proj,
    )
    moment_new, second_new, master_new, proposal = pl.pallas_call(
        result_kernel,
        out_shape=[jax.ShapeDtypeStruct(moment.shape, f32)] * 3
        + [jax.ShapeDtypeStruct((nodes, columns), bf16)],
        in_specs=[hbm] * 6,
        out_specs=[hbm] * 4,
        scratch_shapes=[
            pltpu.VMEM((2, chunks, rows, width), bf16),
            pltpu.VMEM((2, nodes, rows), bf16),
            pltpu.VMEM((4, 1, columns), f32),
            pltpu.VMEM((3, 1, columns), f32),
            pltpu.VMEM((2, chunks, nodes, width), bf16),
            dma((5 + 2 * chunks,)),
            dma((3 + 2 * chunks,)),
        ],
        compiler_params=pltpu.CompilerParams(vmem_limit_bytes=limit),
    )(roll, hidden, g_row, moment, second, master)
    return (moment_new, second_new, master_new, proposal.reshape(1, nodes, columns))


def solution(mesh):
    in_specs = (
        P("fsdp", None),
        P("fsdp", "tp"),
        P("fsdp", "tp"),
        P("fsdp", "tp"),
        P("fsdp", "tp"),
        P("fsdp", None, "tp", None),
        P("fsdp", None, "tp", None),
        P("fsdp", None, "tp", None),
        P("fsdp", None, "tp", None),
        P("fsdp", None, "tp", None),
        P("fsdp", None),
        P("fsdp"),
        P("fsdp", None, None),
        P("tp", None),
    )
    out_specs = (P("fsdp", "tp"), P("fsdp", "tp"), P("fsdp", "tp"), P("fsdp", None, "tp"))
    body = functools.partial(local, grid=GRIDS[mesh.shape["fsdp"]], nt=mesh.shape["tp"])
    return jax.shard_map(body, mesh=mesh, in_specs=in_specs, out_specs=out_specs, check_vma=False)
```

```python
import functools

import jax
import jax.numpy as jnp
from jax import lax
from jax.experimental import pallas as pl
from jax.experimental.pallas import tpu as pltpu
from jax.sharding import PartitionSpec as P

beta_one = 0.9
beta_two = 0.95
adam_eps = 1e-08
learn_rate = 0.001
weight_decay = 0.1
adam_count = 10
masked_score = -1e30

MESH = pl.DeviceIdType.MESH
LANES = 128
GRIDS = {128: (8, 8, 2)}


def nt_dot(a, b):
    return lax.dot_general(a, b, (((1,), (1,)), ((), ())), preferred_element_type=jnp.float32)


def dot(a, b):
    return jnp.dot(a, b, preferred_element_type=jnp.float32)


def adam(g, moment, second, master):
    moment_new = beta_one * moment + (1.0 - beta_one) * g
    second_new = beta_two * second + (1.0 - beta_two) * g * g
    corr_one = 1.0 - beta_one**adam_count
    corr_two = 1.0 - beta_two**adam_count
    direction = moment_new / corr_one / (jnp.sqrt(second_new / corr_two) + adam_eps)
    master_new = master - learn_rate * (direction + weight_decay * master)
    return moment_new, second_new, master_new


def step_kernel(
    cfg,
    acts_h,
    og_h,
    mom_h,
    sec_h,
    mas_h,
    q_h,
    k_h,
    v_h,
    tk_h,
    tv_h,
    par_h,
    len_h,
    res_h,
    op_h,
    new_o,
    hid_o,
    roll_o,
    acts,
    og,
    opt,
    opt_t,
    q,
    k,
    v,
    tk,
    tv,
    par,
    length,
    res,
    op,
    grad,
    rs_out,
    rs_in,
    tile_f,
    tile_out,
    tile_in,
    row_all,
    blk,
    relay,
    qf,
    ht,
    ht_in,
    hid,
    opt_new,
    own,
    load_sem,
    store_sem,
    rs_send,
    rs_recv,
    ex_send,
    ex_recv,
    row_send,
    row_recv,
    ag_send,
    ag_recv,
    tp_send,
    tp_recv,
):
    nx, ny, nz, nt, chunks = cfg
    rows = acts.shape[1]
    width = grad.shape[-1]
    per = width // LANES
    tiles = per * chunks
    pad = tile_out.shape[2]
    nodes = res.shape[0]
    heads = q.shape[0] // nodes
    legs = nt.bit_length() - 1

    f = lax.axis_index("fsdp")
    t = lax.axis_index("tp")
    x, y, z = f // (ny * nz), lax.rem(f // nz, ny), lax.rem(f, nz)
    sides = (nx, ny)
    pos = (x, y)
    group = (ny * nz, nx * nz)
    mine = (y * nz + z, x * nz + z)

    def line_peer(a, at):
        if a == 0:
            return (at * ny + y) * nz + z
        return (x * ny + at) * nz + z

    def group_peer(a, j):
        if a == 0:
            return x * (ny * nz) + j
        return ((j // nz) * ny + y) * nz + lax.rem(j, nz)

    def across(leg):
        step = 1 << leg
        return t + step - 2 * step * lax.rem(t // step, 2)

    def far_first(n):
        return sorted(range(1, n), key=lambda kk: -min(kk, n - kk))

    loads = {}

    def load(name, src, dst):
        copy = pltpu.make_async_copy(src, dst, load_sem.at[len(loads)])
        copy.start()
        loads[name] = copy

    load("acts", acts_h, acts)
    for c in range(chunks):
        for a in range(2):
            base = (a * chunks + c) * width
            load(("og", a, c), og_h.at[:, pl.ds(base, width)], og.at[a, c])

    barrier = pltpu.get_barrier_semaphore()
    count = 0
    for a in range(2):
        for kk in far_first(sides[a]):
            peer = line_peer(a, lax.rem(pos[a] + kk, sides[a]))
            pl.semaphore_signal(barrier, inc=1, device_id=(peer, t), device_id_type=MESH)
            count += 1
    for zz in range(1, nz):
        peer = (x * ny + y) * nz + lax.rem(z + zz, nz)
        pl.semaphore_signal(barrier, inc=1, device_id=(peer, t), device_id_type=MESH)
        count += 1
    for leg in range(legs):
        pl.semaphore_signal(barrier, inc=1, device_id=(f, across(leg)), device_id_type=MESH)
        count += 1

    row_at = lax.broadcasted_iota(jnp.int32, (rows, rows), 0)
    col_at = lax.broadcasted_iota(jnp.int32, (rows, rows), 1)
    py, px, pz = row_at // (nx * nz), lax.rem(row_at // nz, nx), lax.rem(row_at, nz)
    swap = (col_at == (px * ny + py) * nz + pz).astype(jnp.bfloat16)
    same = (col_at == row_at).astype(jnp.bfloat16)
    loads["acts"].wait()
    acts_t = [nt_dot(m, acts[...]).astype(jnp.bfloat16) for m in (same, swap)]

    def block(a, at):
        depth = rows // sides[a]
        return pl.ds(pl.multiple_of(at * depth, depth), depth)

    def wait_for(ref, sem):
        pltpu.make_async_copy(ref, ref, sem).wait()

    for c in range(chunks):
        for a in range(2):
            n = sides[a]
            loads[("og", a, c)].wait()
            value = dot(acts_t[a], og[a, c])
            grad[a, c] = value
            rs_out[a, c] = value.astype(jnp.bfloat16)
            if c == 0 and a == 0:
                pl.semaphore_wait(barrier, count)
            for kk in far_first(n):
                at = lax.rem(pos[a] + kk, n)
                pltpu.make_async_remote_copy(
                    src_ref=rs_out.at[a, c, block(a, at)],
                    dst_ref=rs_in.at[a, c, kk - 1],
                    send_sem=rs_send.at[a, c],
                    recv_sem=rs_recv.at[a, c],
                    device_id=(line_peer(a, at), t),
                    device_id_type=MESH,
                ).start()

    load("par", par_h, par)
    load("q", q_h, q)
    load("tk", tk_h, tk)
    load("k", k_h, k)
    load("len", len_h, length)
    load("v", v_h, v)
    load("tv", tv_h, tv)
    load("op", op_h, op)
    load("mom", mom_h, opt.at[0])
    load("sec", sec_h, opt.at[1])
    load("mas", mas_h, opt.at[2])
    load("res", res_h, res)
    tile_f[...] = jnp.zeros_like(tile_f)

    loads["par"].wait()
    j_at = lax.broadcasted_iota(jnp.int32, (nodes, nodes), 0)
    i_at = lax.broadcasted_iota(jnp.int32, (nodes, nodes), 1)
    links = ((par[...] == j_at) & (i_at > 0)) | (i_at == j_at)
    reach = links.astype(jnp.bfloat16)
    for _ in range(max(1, (nodes - 1).bit_length())):
        reach = jnp.minimum(dot(reach, reach), 1.0).astype(jnp.bfloat16)
    pick_row = lax.broadcasted_iota(jnp.int32, (2 * nodes, nodes), 0)
    pick_col = lax.broadcasted_iota(jnp.int32, (2 * nodes, nodes), 1)
    pick = (lax.rem(pick_row, nodes) == pick_col).astype(jnp.bfloat16)
    admitted = nt_dot(pick, reach) > 0.5
    loads["q"].wait()
    qf[...] = q[...].astype(jnp.float32)

    depth = q.shape[1]
    scale = depth ** (-0.5)
    for name in ("tk", "k", "len", "v", "tv", "op"):
        loads[name].wait()

    def attend(u):
        pair = jnp.concatenate(
            [qf[pl.ds(2 * u + e, nodes, stride=heads), :] for e in range(2)], axis=0
        ).astype(jnp.bfloat16)
        s_cache = nt_dot(pair, k[...])
        s_tree = nt_dot(pair, tk[...])
        live = lax.broadcasted_iota(jnp.int32, s_cache.shape, 1) < length[...]
        s_cache = jnp.where(live, s_cache, masked_score)
        s_tree = jnp.where(admitted, s_tree, masked_score)
        top = jnp.maximum(
            jnp.max(s_cache, axis=1, keepdims=True), jnp.max(s_tree, axis=1, keepdims=True)
        )
        e_cache = jnp.exp((s_cache - top) * scale)
        e_tree = jnp.exp((s_tree - top) * scale)
        total = jnp.sum(e_cache, axis=1, keepdims=True) + jnp.sum(e_tree, axis=1, keepdims=True)
        mixed = dot(e_cache.astype(jnp.bfloat16), v[...]) + dot(e_tree.astype(jnp.bfloat16), tv[...])
        mixed = (mixed / total).astype(jnp.bfloat16)
        add = dot(mixed[:nodes], op[pl.ds(2 * u * depth, depth), :]) + dot(
            mixed[nodes:], op[pl.ds((2 * u + 1) * depth, depth), :]
        )
        if u == 0:
            ht[0] = add
        else:
            ht[0] += add

    units = heads // 2
    early = units - 1
    for u in range(early):
        attend(u)

    for i, name in enumerate(("mom", "sec", "mas")):
        loads[name].wait()
        for a in range(2):
            for e in range(tiles):
                opt_t[i, a, pl.ds(e, 1), :] = opt[i, :, pl.ds((a * tiles + e) * LANES, LANES)]
    loads["res"].wait()

    wait_for(rs_in.at[1, 0], rs_recv.at[1, 0])
    for a in range(2):
        n = sides[a]
        for c in range(chunks):
            if (a, c) != (1, 0):
                wait_for(rs_in.at[a, c], rs_recv.at[a, c])
            value = grad[a, c, block(a, pos[a]), :]
            for kk in range(n - 1):
                value = value + rs_in[a, c, kk].astype(jnp.float32)
            for e in range(per):
                tile_f[a, pl.ds(c * per + e, group[a], stride=pad), :] = value[:, e * LANES : (e + 1) * LANES]
        tile_out[a] = tile_f[a].astype(jnp.bfloat16).reshape(group[a], pad, LANES)
        for kk in far_first(group[a]):
            j = lax.rem(mine[a] + kk, group[a])
            pltpu.make_async_remote_copy(
                src_ref=tile_out.at[a, j],
                dst_ref=tile_in.at[a, kk - 1],
                send_sem=ex_send.at[a],
                recv_sem=ex_recv.at[a],
                device_id=(group_peer(a, j), t),
                device_id_type=MESH,
            ).start()
        own[a] = tile_f[a, pl.ds(pl.multiple_of(mine[a] * pad, pad), pad), :]

    for u in range(early, units):
        attend(u)

    leg_copies = []

    def leg_start(leg):
        copy = pltpu.make_async_remote_copy(
            src_ref=ht.at[leg],
            dst_ref=ht_in.at[leg],
            send_sem=tp_send.at[leg],
            recv_sem=tp_recv.at[leg],
            device_id=(f, across(leg)),
            device_id_type=MESH,
        )
        copy.start()
        leg_copies.append(copy)

    def leg_end(leg):
        leg_copies[leg].wait_recv()
        ht[leg + 1] = ht[leg] + ht_in[leg]
        if leg + 1 < legs:
            leg_start(leg + 1)

    leg_start(0)

    fresh = []
    for a in range(2):
        wait_for(tile_in.at[a], ex_recv.at[a])
        g = own[a]
        for kk in range(group[a] - 1):
            g = g + tile_in[a, kk].astype(jnp.float32)
        g = g[:tiles]
        fresh.append(adam(g, opt_t[0, a], opt_t[1, a], opt_t[2, a]))
        master_new = fresh[a][2]
        if pad > tiles:
            fill = jnp.zeros((pad - tiles, LANES), jnp.float32)
            master_new = jnp.concatenate([master_new, fill], axis=0)
        row_all[a, mine[a]] = master_new.astype(jnp.bfloat16)
        for kk in far_first(group[a]):
            j = lax.rem(mine[a] + kk, group[a])
            pltpu.make_async_remote_copy(
                src_ref=row_all.at[a, mine[a]],
                dst_ref=row_all.at[a, mine[a]],
                send_sem=row_send.at[a],
                recv_sem=row_recv.at[a],
                device_id=(group_peer(a, j), t),
                device_id_type=MESH,
            ).start()

    stores = []

    def store(src, dst):
        copy = pltpu.make_async_copy(src, dst, store_sem.at[len(stores)])
        copy.start()
        stores.append(copy)


    leg_end(0)

    ag_copies = []

    def ag_copy(a, c, d, kind, src, owner, step):
        n = sides[a]
        at = lax.rem(pos[a] + (1 - 2 * d) * step + n, n)
        landing = relay.at[a, c, d] if kind == 1 else roll_o.at[a, c, block(a, owner)]
        return pltpu.make_async_remote_copy(
            src_ref=src,
            dst_ref=landing,
            send_sem=ag_send.at[a, c, d, kind],
            recv_sem=ag_recv.at[a, c, d, kind],
            device_id=(line_peer(a, at), t),
            device_id_type=MESH,
        )

    def ag_start(*which):
        copy = ag_copy(*which)
        copy.start()
        ag_copies.append(copy)

    for a in range(2):
        wait_for(row_all.at[a, pl.ds(0, group[a] - 1)], row_recv.at[a])
        tile_f[a] = row_all[a].astype(jnp.float32).reshape(group[a] * pad, LANES)
        for c in range(chunks):
            for e in range(per):
                blk[a, c, :, pl.ds(e * LANES, LANES)] = tile_f[
                    a, pl.ds(c * per + e, group[a], stride=pad), :
                ].astype(jnp.bfloat16)
            for d in range(2):
                ag_start(a, c, d, 1, blk.at[a, c], pos[a], 2)
        for c in range(chunks):
            for d in range(2):
                ag_start(a, c, d, 0, blk.at[a, c], pos[a], 1)
            store(blk.at[a, c], roll_o.at[a, c, block(a, pos[a])])
    for i in range(3):
        for a in range(2):
            for e in range(tiles):
                opt_new[i, :, pl.ds((a * tiles + e) * LANES, LANES)] = fresh[a][i][e : e + 1]
    store(opt_new, new_o)
    if legs > 1:
        leg_end(1)
    for a in range(2):
        n = sides[a]
        for c in range(chunks):
            for d in range(2):
                owner = lax.rem(pos[a] - 2 * (1 - 2 * d) + n, n)
                ag_copy(a, c, d, 1, blk.at[a, c], pos[a], 2).wait_recv()
                ag_start(a, c, d, 2, relay.at[a, c, d], owner, 1)
                if c % 2 == d:
                    ag_start(a, c, d, 3, relay.at[a, c, d], owner, 2)
                store(relay.at[a, c, d], roll_o.at[a, c, block(a, owner)])

    for leg in range(2, legs):
        leg_end(leg)
    hidden = (res[...].astype(jnp.float32) + ht[legs]).astype(jnp.bfloat16)
    hid[0] = hidden
    hid[1] = nt_dot(hidden, swap).astype(jnp.bfloat16)
    store(hid, hid_o)

    for a in range(2):
        for c in range(chunks):
            wait_for(rs_in.at[a, c], rs_send.at[a, c])
        wait_for(tile_in.at[a], ex_send.at[a])
        wait_for(row_all.at[a, pl.ds(0, group[a] - 1)], row_send.at[a])
    for copy in leg_copies:
        copy.wait_send()
    for copy in stores:
        copy.wait()
    for copy in ag_copies:
        copy.wait_send()
    for a in range(2):
        for c in range(chunks):
            for d in range(2):
                for kind in (0, 2, 3):
                    if kind < 3 or c % 2 == d:
                        ag_copy(a, c, d, kind, blk.at[a, c], pos[a], 1).wait_recv()


def result_kernel(
    roll_h, hid_h, new_h, mom_o, sec_o, mas_o, prop_o, roll, hid, stage, load_sem, store_sem
):
    halves, chunks, _, width = roll.shape
    parts = halves * chunks
    pairs = [(hid_h, hid)]
    for i in range(parts):
        at = (i // chunks, i % chunks)
        pairs.append((roll_h.at[at], roll.at[at]))
    loads = [pltpu.make_async_copy(src, dst, load_sem.at[i]) for i, (src, dst) in enumerate(pairs)]
    for copy in loads:
        copy.start()
    stores = []

    def store(src, dst):
        copy = pltpu.make_async_copy(src, dst, store_sem.at[len(stores)])
        copy.start()
        stores.append(copy)

    for i, ref in enumerate((mom_o, sec_o, mas_o)):
        store(new_h.at[i], ref)
    loads[0].wait()
    for i in range(parts):
        a, c = i // chunks, i % chunks
        loads[1 + i].wait()
        stage[a, c] = dot(hid[a], roll[a, c]).astype(jnp.bfloat16)
        store(stage.at[a, c], prop_o.at[:, pl.ds(i * width, width)])
    for copy in stores:
        copy.wait()


def local(
    acts,
    out_grad,
    moment,
    second,
    master,
    queries,
    cache_keys,
    cache_values,
    tree_keys,
    tree_values,
    parents,
    lengths,
    residual,
    out_proj,
    *,
    grid,
    nt,
):
    nx, ny, nz = grid
    chunks = 2
    rows = acts.shape[1]
    columns = out_grad.shape[1]
    width = columns // (2 * chunks)
    tiles = width // LANES * chunks
    pad = -(-tiles // 16) * 16
    nodes, heads, depth = queries.shape[1:]
    cache = cache_keys.shape[1]
    side = ny * nz
    legs = nt.bit_length() - 1
    bf16, f32 = jnp.bfloat16, jnp.float32
    hbm = pl.BlockSpec(memory_space=pltpu.HBM)
    dma = pltpu.SemaphoreType.DMA
    limit = 56 * 1024 * 1024
    new_rows, hidden, roll = pl.pallas_call(
        functools.partial(step_kernel, (nx, ny, nz, nt, chunks)),
        out_shape=[
            jax.ShapeDtypeStruct((3, 1, columns), f32),
            jax.ShapeDtypeStruct((2, nodes, rows), bf16),
            jax.ShapeDtypeStruct((2, chunks, rows, width), bf16),
        ],
        in_specs=[hbm] * 14,
        out_specs=[hbm] * 3,
        scratch_shapes=[
            pltpu.VMEM(acts.shape, bf16),
            pltpu.VMEM((2, chunks, acts.shape[0], width), bf16),
            pltpu.VMEM((3, 1, columns), f32),
            pltpu.VMEM((3, 2, tiles, LANES), f32),
            pltpu.VMEM((nodes * heads, depth), bf16),
            pltpu.VMEM((cache, depth), bf16),
            pltpu.VMEM((cache, depth), bf16),
            pltpu.VMEM((nodes, depth), bf16),
            pltpu.VMEM((nodes, depth), bf16),
            pltpu.VMEM((1, nodes), jnp.int32),
            pltpu.VMEM((1, 1), jnp.int32),
            pltpu.VMEM((nodes, rows), bf16),
            pltpu.VMEM(out_proj.shape, bf16),
            pltpu.VMEM((2, chunks, rows, width), f32),
            pltpu.VMEM((2, chunks, rows, width), bf16),
            pltpu.VMEM((2, chunks, nx - 1, side, width), bf16),
            pltpu.VMEM((2, side * pad, LANES), f32),
            pltpu.VMEM((2, side, pad, LANES), bf16),
            pltpu.VMEM((2, side - 1, pad, LANES), bf16),
            pltpu.VMEM((2, side, pad, LANES), bf16),
            pltpu.VMEM((2, chunks, side, width), bf16),
            pltpu.VMEM((2, chunks, 2, side, width), bf16),
            pltpu.VMEM((nodes * heads, depth), f32),
            pltpu.VMEM((legs + 1, nodes, rows), f32),
            pltpu.VMEM((legs, nodes, rows), f32),
            pltpu.VMEM((2, nodes, rows), bf16),
            pltpu.VMEM((3, 1, columns), f32),
            pltpu.VMEM((2, pad, LANES), f32),
            dma((13 + 2 * chunks,)),
            dma((2 + 6 * chunks,)),
            dma((2, chunks)),
            dma((2, chunks)),
            dma((2,)),
            dma((2,)),
            dma((2,)),
            dma((2,)),
            dma((2, chunks, 2, 4)),
            dma((2, chunks, 2, 4)),
            dma((legs,)),
            dma((legs,)),
        ],
        compiler_params=pltpu.CompilerParams(
            collective_id=0, has_side_effects=True, vmem_limit_bytes=limit
        ),
    )(
        acts,
        out_grad,
        moment,
        second,
        master,
        queries.reshape(nodes * heads, depth),
        cache_keys.reshape(cache, depth),
        cache_values.reshape(cache, depth),
        tree_keys.reshape(nodes, depth),
        tree_values.reshape(nodes, depth),
        parents,
        lengths.reshape(1, 1),
        residual.reshape(nodes, rows),
        out_proj,
    )
    moment_new, second_new, master_new, proposal = pl.pallas_call(
        result_kernel,
        out_shape=[jax.ShapeDtypeStruct(moment.shape, f32)] * 3
        + [jax.ShapeDtypeStruct((nodes, columns), bf16)],
        in_specs=[hbm] * 3,
        out_specs=[hbm] * 4,
        scratch_shapes=[
            pltpu.VMEM((2, chunks, rows, width), bf16),
            pltpu.VMEM((2, nodes, rows), bf16),
            pltpu.VMEM((2, chunks, nodes, width), bf16),
            dma((1 + 2 * chunks,)),
            dma((3 + 2 * chunks,)),
        ],
        compiler_params=pltpu.CompilerParams(vmem_limit_bytes=limit),
    )(roll, hidden, new_rows)
    return (moment_new, second_new, master_new, proposal.reshape(1, nodes, columns))


def solution(mesh):
    in_specs = (
        P("fsdp", None),
        P("fsdp", "tp"),
        P("fsdp", "tp"),
        P("fsdp", "tp"),
        P("fsdp", "tp"),
        P("fsdp", None, "tp", None),
        P("fsdp", None, "tp", None),
        P("fsdp", None, "tp", None),
        P("fsdp", None, "tp", None),
        P("fsdp", None, "tp", None),
        P("fsdp", None),
        P("fsdp"),
        P("fsdp", None, None),
        P("tp", None),
    )
    out_specs = (P("fsdp", "tp"), P("fsdp", "tp"), P("fsdp", "tp"), P("fsdp", None, "tp"))
    body = functools.partial(local, grid=GRIDS[mesh.shape["fsdp"]], nt=mesh.shape["tp"])
    return jax.shard_map(body, mesh=mesh, in_specs=in_specs, out_specs=out_specs, check_vma=False)
```
